512 devices in a mesh: dom: 512 (over y, x, z, core).
Axes of the slice: x: 4, y: 8, z: 8, core: 2. Of those that a mesh axis runs over, the one named last changes fastest.
Arguments:
- base_cell: int32 [2097152], P('dom'), may hold values from 0 to 63
- offset: float32 [3, 2097152], P(None, 'dom'), may hold values from 0 to 1
- velocity: float32 [3, 2097152], P(None, 'dom'), may hold values from -4 to 4
- affine: float32 [9, 2097152], P(None, 'dom'), may hold values from -3 to 3
- strain: float32 [9, 2097152], P(None, 'dom'), may hold values from -0.1 to 0.1
- plastic: float32 [2097152], P('dom'), may hold values from 0.9 to 1.1
- particle_mass: float32 [2097152], P('dom'), may hold values from 0.5 to 2
- counts: int32 [8192], P('dom'), may hold values from 8 to 256, as said below
- neighbours: int32 [8192, 27], P('dom'), may hold values from -1 to 111, as said below
- send_rows: int32 [512, 96], P('dom'), may hold values from 0 to 15
Outputs:
- final_offset: float32 [3, 2097152], P(None, 'dom')
- final_velocity: float32 [3, 2097152], P(None, 'dom')
- final_affine: float32 [9, 2097152], P(None, 'dom')
- final_deform: float32 [9, 2097152], P(None, 'dom')
- final_plastic: float32 [2097152], P('dom')
The draws below stay inside these ranges and needn't reach their ends.
Inputs may be any that keep to these rules, and one draw needn't show every extreme that they name: `counts`: partitions differ in density by up to a factor of four; some block holds exactly 256 particles in every draw. `neighbours`: column 13 holds each block's own index among its partition's 16 blocks; every received border block is named somewhere by its partition; -1 means no neighbour.
All inputs are finite; a program needn't handle non-finite values.
Results may differ from the reference program's by a relative error of at most 0.0003.
Values sent between devices are 32-bit elements; how exact they have to be, the bound alone decides.
A program may use at most 64 MiB of HBM per device.

```python
import math
import jax
import jax.numpy as jnp
from jax import lax

OWN = 16
PMAX = 256
HOPS = 4
SLOTS = 12
BLOCKS = 8192
PARTS_SIZE = 2097152
N_DOM = 512


def draw_counts(key, part):
    key = jax.random.fold_in(key, 11)
    partitions = BLOCKS // OWN
    key_base = jax.random.fold_in(key, 1)
    key_pick = jax.random.fold_in(key, 2)
    key_dense = jax.random.fold_in(key, 3)
    key_full = jax.random.fold_in(key, 4)
    lowest = max(PMAX // 32, 1)
    base = jax.random.randint(key_base, (BLOCKS,), lowest, PMAX // 4 + 1)
    pick = jax.random.randint(key_pick, (partitions,), 0, 4)
    dense = jax.random.randint(key_dense, (), 0, partitions)
    heavy = (pick == 3) | (jnp.arange(partitions, dtype=jnp.int32) == dense)
    factor = jnp.where(heavy, 4, 1)
    filled = jnp.minimum(base * jnp.repeat(factor, OWN), PMAX)
    chosen = jax.random.randint(key_full, (partitions,), 0, OWN)
    local = jnp.arange(BLOCKS, dtype=jnp.int32) % OWN
    is_full = jnp.repeat(heavy, OWN) & (local == jnp.repeat(chosen, OWN))
    return jnp.where(is_full, PMAX, filled).astype(jnp.int32)


def draw_neighbours(key, part):
    key = jax.random.fold_in(key, 23)
    received = 2 * HOPS * SLOTS
    raw = jax.random.randint(key, (BLOCKS, 27), -1, OWN + received)
    local = (jnp.arange(BLOCKS, dtype=jnp.int32) % OWN)[:, None]
    column = jnp.arange(27, dtype=jnp.int32)[None, :]
    target = column * OWN + local
    forced = (column < 13) & (target < received)
    table = jnp.where(forced, OWN + target, raw)
    table = jnp.where((column == 26) & (local == OWN - 1), -1, table)
    return jnp.where(column == 13, local, table).astype(jnp.int32)


def with_ends(values, key, smallest, top_value):
    longest = values.shape.index(max(values.shape))
    spots = []
    for shift in (0, 1):
        where = [jax.random.randint(jax.random.fold_in(key, axis), (), 0, length) for axis, length in enumerate(values.shape)]
        where[longest] = (where[longest] + shift) % values.shape[longest]
        spots.append(tuple(where))
    return values.at[spots[0]].set(smallest).at[spots[1]].set(top_value)


def block_levels(key, extent, cuts, smallest, top_value):
    loudness = 1.0
    for position, blocks in cuts:
        steps = jax.random.uniform(jax.random.fold_in(jax.random.fold_in(key, 6), position), (blocks,), jnp.float32, smallest / len(cuts), top_value / len(cuts))
        loudness = loudness * jnp.repeat(jnp.exp(steps), extent[position] // blocks).reshape((-1,) + (1,) * (len(extent) - 1 - position))
    return loudness


def noise(rng, shape, width, limit, split=(), kind=jnp.bfloat16):
    gain = block_levels(rng, shape, split, -0.22, 0.18) if split else 1.0
    drawn = jax.random.normal(rng, shape, jnp.float32) * width * gain
    return jnp.minimum(jnp.maximum(drawn, -limit), limit).astype(kind)


def setup_inputs(seed: int = 0) -> dict:
    splits = jax.random.split(jax.random.key(seed), 11)
    base_cell = with_ends(jax.random.randint(splits[0], (PARTS_SIZE,), 0, 64), jax.random.fold_in(splits[0], 1), 0, 63).astype(jnp.int32)
    offset = jnp.clip(1.0 * jax.random.uniform(splits[1], (3, PARTS_SIZE), jnp.float32) ** block_levels(splits[1], (3, PARTS_SIZE), ((1, 512),), -0.2, 0.2), 0.0, 1.0)
    velocity = noise(splits[2], (3, PARTS_SIZE), 1.0, 4.0, ((1, 512),), jnp.float32)
    affine = noise(splits[3], (9, PARTS_SIZE), 0.5, 3.0, ((1, 512),), jnp.float32)
    strain = jnp.clip(jax.random.uniform(splits[4], (9, PARTS_SIZE), jnp.float32, -0.1, 0.1) * block_levels(splits[4], (9, PARTS_SIZE), ((1, 512),), -0.4, 0.0), -0.1, 0.1)
    plastic = jnp.clip(jnp.exp(math.log(1.1) - 0.200670744 * jax.random.uniform(splits[5], (PARTS_SIZE,), jnp.float32) ** block_levels(splits[5], (PARTS_SIZE,), ((0, 512),), -0.2, 0.2)), 0.9, 1.1)
    particle_mass = jnp.clip(jnp.exp(math.log(2.0) - 1.3862944 * jax.random.uniform(splits[6], (PARTS_SIZE,), jnp.float32) ** block_levels(splits[6], (PARTS_SIZE,), ((0, 512),), -0.2, 0.2)), 0.5, 2.0)
    counts = draw_counts(jax.random.fold_in(splits[10], 71), 0)
    neighbours = draw_neighbours(jax.random.fold_in(splits[10], 71), 0)
    send_rows = with_ends(jax.random.randint(splits[9], (N_DOM, 2 * HOPS * SLOTS), 0, OWN), jax.random.fold_in(splits[9], 1), 0, OWN - 1).astype(jnp.int32)
    return dict(base_cell=base_cell, offset=offset, velocity=velocity, affine=affine, strain=strain, plastic=plastic, particle_mass=particle_mass, counts=counts, neighbours=neighbours, send_rows=send_rows)


DT = 0.05
SHEAR = 4.0
BULK = 4.0
HARDEN = 10.0
COMPRESS = 0.025
STRETCH = 0.0075
DENSITY = 1.0
GRAVITY = 1.0
MASS_FLOOR = 0.25
SOURCE_RIM = ((5, 6), (1, 5), (0, 1))
PAD_CORE = ((0, 3), (0, 0), (3, 0))
SOURCE_CORE = ((3, 4), (0, 4), (0, 1))
PAD_RIM = ((0, 5), (1, 1), (5, 0))


def determinant(matrix):
    return (matrix[0] * (matrix[4] * matrix[8] - matrix[5] * matrix[7])
            - matrix[1] * (matrix[3] * matrix[8] - matrix[5] * matrix[6])
            + matrix[2] * (matrix[3] * matrix[7] - matrix[4] * matrix[6]))


def project(deform, plastic):
    volume = determinant(deform)
    clamped = jnp.clip(volume, 1.0 - COMPRESS, 1.0 + STRETCH)
    hardened = plastic * volume / clamped
    factor = jnp.exp(jnp.log(clamped / volume) / 3.0)
    return deform * factor[None], hardened, clamped


def kirchhoff(elastic, hardened, clamped):
    factor = jnp.exp(HARDEN * (1.0 - hardened))
    shear = SHEAR * factor
    bulk = BULK * factor * jnp.log(clamped)
    entries = []
    for i in range(3):
        for j in range(3):
            inner = elastic[3 * i] * elastic[3 * j] + elastic[3 * i + 1] * elastic[3 * j + 1] + elastic[3 * i + 2] * elastic[3 * j + 2]
            if i == j:
                entries.append(shear * (inner - 1.0) + bulk)
            else:
                entries.append(shear * inner)
    return jnp.stack(entries)


def coordinates(cells):
    return (cells // 16, (cells // 4) % 4, cells % 4)


def particle_positions(cells, offset):
    corner = coordinates(cells)
    return jnp.stack([corner[i].astype(jnp.float32) + 0.5 + offset[i] for i in range(3)])


def spline(cells, offset):
    corner = coordinates(cells)
    places = jnp.arange(6, dtype=jnp.int32)
    tables = []
    for i in range(3):
        frac = 0.5 + offset[i]
        first = 0.5 * (1.5 - frac) * (1.5 - frac)
        second = 0.75 - (frac - 1.0) * (frac - 1.0)
        third = 0.5 * (frac - 0.5) * (frac - 0.5)
        shift = places[None, None, :] - corner[i][:, :, None]
        table = (jnp.where(shift == 0, first[:, :, None], 0.0)
                 + jnp.where(shift == 1, second[:, :, None], 0.0)
                 + jnp.where(shift == 2, third[:, :, None], 0.0))
        tables.append(table)
    weights = tables[0][:, :, :, None, None] * tables[1][:, :, None, :, None] * tables[2][:, :, None, None, :]
    return weights.reshape(cells.shape + (216,))


def node_positions():
    index = jnp.arange(216, dtype=jnp.int32)
    return jnp.stack([index // 36, (index // 6) % 6, index % 6]).astype(jnp.float32)


def particle_values(mass, velocity, affine, stress, positions, live):
    volume = mass / DENSITY
    impulse = [-(4.0 * DT) * volume * stress[i] + mass * affine[i] for i in range(9)]
    carried = []
    for i in range(3):
        carried.append(mass * velocity[i] - impulse[3 * i] * positions[0] - impulse[3 * i + 1] * positions[1] - impulse[3 * i + 2] * positions[2])
    values = jnp.stack([mass] + carried + impulse)
    return jnp.where(live[None], values, 0.0)


def scatter_blocks(cells, offset, values, nodes):
    weights = spline(cells, offset)
    sums = jnp.einsum("cbp,bpj->bcj", values, weights, precision=lax.Precision.HIGHEST)
    moments = []
    for i in range(3):
        total = sums[:, 1 + i]
        for j in range(3):
            total = total + sums[:, 4 + 3 * i + j] * nodes[j][None]
        moments.append(total)
    return jnp.stack([sums[:, 0]] + moments, axis=1)


def gather_particles(cells, offset, padded, nodes):
    weights = spline(cells, offset)
    positions = particle_positions(cells, offset)
    columns = [padded[:, i] for i in range(3)]
    for i in range(3):
        for j in range(3):
            columns.append(padded[:, i] * nodes[j][None])
    stacked = jnp.stack(columns, axis=1)
    result = jnp.einsum("bpj,bcj->bcp", weights, stacked, precision=lax.Precision.HIGHEST)
    speeds = result[:, 0:3]
    entries = []
    for i in range(3):
        for j in range(3):
            entries.append(4.0 * (result[:, 3 + 3 * i + j] - speeds[:, i] * positions[j]))
    return jnp.concatenate([speeds, jnp.stack(entries, axis=1)], axis=1)


def assemble_core(fetch):
    total = 0.0
    for index in range(27):
        steps = (index // 9, (index // 3) % 3, index % 3)
        piece = fetch(index)
        piece = piece.reshape(piece.shape[:2] + (6, 6, 6))
        piece = piece[:, :, SOURCE_RIM[steps[0]][0]:SOURCE_RIM[steps[0]][1],
                      SOURCE_RIM[steps[1]][0]:SOURCE_RIM[steps[1]][1],
                      SOURCE_RIM[steps[2]][0]:SOURCE_RIM[steps[2]][1]]
        piece = jnp.pad(piece, ((0, 0), (0, 0), PAD_CORE[steps[0]], PAD_CORE[steps[1]], PAD_CORE[steps[2]]))
        total = total + piece
    return total.reshape(total.shape[:2] + (64,))


def assemble_padded(fetch):
    total = 0.0
    for index in range(27):
        steps = (index // 9, (index // 3) % 3, index % 3)
        piece = fetch(index)
        piece = piece.reshape(piece.shape[:2] + (4, 4, 4))
        piece = piece[:, :, SOURCE_CORE[steps[0]][0]:SOURCE_CORE[steps[0]][1],
                      SOURCE_CORE[steps[1]][0]:SOURCE_CORE[steps[1]][1],
                      SOURCE_CORE[steps[2]][0]:SOURCE_CORE[steps[2]][1]]
        piece = jnp.pad(piece, ((0, 0), (0, 0), PAD_RIM[steps[0]], PAD_RIM[steps[1]], PAD_RIM[steps[2]]))
        total = total + piece
    return total.reshape(total.shape[:2] + (216,))


def node_speeds(totals):
    weight = jnp.maximum(totals[:, 0], MASS_FLOOR)
    down = jnp.array([0.0, 0.0, DT * GRAVITY], dtype=jnp.float32)
    return totals[:, 1:4] / weight[:, None] - down[None, :, None]


def finish(state, elastic, hardened, result, live):
    offset, velocity, affine, deform, plastic = state
    new_velocity = result[0:3]
    new_affine = result[3:12]
    new_offset = offset + DT * new_velocity
    entries = []
    for i in range(3):
        for j in range(3):
            total = elastic[3 * i + j]
            for k in range(3):
                total = total + DT * new_affine[3 * i + k] * elastic[3 * k + j]
            entries.append(total)
    new_deform = jnp.stack(entries)
    keep = live[None]
    return (jnp.where(keep, new_offset, offset), jnp.where(keep, new_velocity, velocity),
            jnp.where(keep, new_affine, affine), jnp.where(keep, new_deform, deform),
            jnp.where(live, hardened, plastic))


def global_links(neighbours, send_rows):
    blocks = neighbours.shape[0]
    partitions = blocks // OWN
    received = 2 * HOPS * SLOTS
    device = (jnp.arange(blocks, dtype=jnp.int32) // OWN)[:, None]
    remote = jnp.clip(neighbours - OWN, 0, received - 1)
    group = remote // SLOTS
    distance = jnp.where(group < HOPS, group + 1, group - HOPS + 1)
    source = jnp.where(group < HOPS, device - distance, device + distance)
    inside = (source >= 0) & (source < partitions)
    source = jnp.clip(source, 0, partitions - 1)
    listed = send_rows.reshape(-1)[source * received + remote]
    is_own = (neighbours >= 0) & (neighbours < OWN)
    is_remote = (neighbours >= OWN) & inside
    target = jnp.where(is_own, device * OWN + neighbours, source * OWN + listed)
    valid = is_own | is_remote
    return jnp.where(valid, target, 0).astype(jnp.int32), valid


def split_partitions(array, axis, partitions):
    shape = array.shape[:axis] + (partitions, array.shape[axis] // partitions) + array.shape[axis + 1:]
    return jnp.moveaxis(array.reshape(shape), axis, 0)


def advance(state, cells, mass, live, links, valid, nodes, partitions):
    offset, velocity, affine, deform, plastic = state
    elastic, hardened, clamped = project(deform, plastic)
    stress = kirchhoff(elastic, hardened, clamped)
    positions = particle_positions(cells, offset)
    values = particle_values(mass, velocity, affine, stress, positions, live)
    partial_value = lax.map(lambda parts: scatter_blocks(parts[0], parts[1], parts[2], nodes),
                      (split_partitions(cells, 0, partitions), split_partitions(offset, 1, partitions),
                       split_partitions(values, 1, partitions)))
    partial_value = partial_value.reshape((-1,) + partial_value.shape[2:])
    totals = assemble_core(lambda index: jnp.where(valid[:, index, None, None], partial_value[links[:, index]], 0.0))
    speeds = node_speeds(totals)
    padded = assemble_padded(lambda index: jnp.where(valid[:, index, None, None], speeds[links[:, index]], 0.0))
    result = lax.map(lambda parts: gather_particles(parts[0], parts[1], parts[2], nodes),
                     (split_partitions(cells, 0, partitions), split_partitions(offset, 1, partitions),
                      split_partitions(padded, 0, partitions)))
    result = jnp.moveaxis(result.reshape((-1,) + result.shape[2:]), 1, 0)
    return finish(state, elastic, hardened, result, live)


def reference(base_cell, offset, velocity, affine, strain, plastic, particle_mass, counts, neighbours, send_rows):
    blocks = counts.shape[0]
    capacity = base_cell.shape[0] // blocks
    partitions = blocks // OWN
    cells = base_cell.reshape(blocks, capacity)
    identity = jnp.eye(3, dtype=jnp.float32).reshape(9)
    state = (offset.reshape(3, blocks, capacity), velocity.reshape(3, blocks, capacity),
             affine.reshape(9, blocks, capacity), strain.reshape(9, blocks, capacity) + identity[:, None, None],
             plastic.reshape(blocks, capacity))
    mass = particle_mass.reshape(blocks, capacity)
    live = jnp.arange(capacity, dtype=jnp.int32)[None, :] < counts[:, None]
    links, valid = global_links(neighbours, send_rows)
    nodes = node_positions()
    for step in range(2):
        state = advance(state, cells, mass, live, links, valid, nodes, partitions)
    total = blocks * capacity
    return (state[0].reshape(3, total), state[1].reshape(3, total), state[2].reshape(9, total),
            state[3].reshape(9, total), state[4].reshape(total))
```

```python
import jax
import jax.numpy as jnp
import numpy as np
from jax import lax
from jax.experimental import pallas as pl
from jax.experimental.pallas import tpu as pltpu
from jax.sharding import PartitionSpec as P

OWN = 16
PMAX = 256
HOPS = 4
SLOTS = 12
GROUPS = 2 * HOPS
RECEIVED = GROUPS * SLOTS
NONE = OWN + RECEIVED
PARTICLES = OWN * PMAX
TILES = PARTICLES // 128

DT = 0.05
SHEAR = 4.0
BULK = 4.0
HARDEN = 10.0
COMPRESS = 0.025
STRETCH = 0.0075
GRAVITY = 1.0
MASS_FLOOR = 0.25


def tables():
    row = np.arange(8)[:, None]
    lane = np.arange(128)[None, :]
    half = row // 4 + 0 * lane
    third = lane // 36 + 0 * row
    place = lane % 36 + 0 * row
    inside = third < 3
    node = [3 * half + third, place // 6, place % 6]
    step = [(x == 0).astype(int) - (x == 5).astype(int) for x in node]
    offset_id = 9 * (step[0] + 1) + 3 * (step[1] + 1) + step[2] + 1
    offset_id = np.where(inside, offset_id, 13)
    core = [(x + 3) % 4 for x in node]
    core_id = np.where(inside, 16 * core[0] + 4 * core[1] + core[2], -1)
    fold = np.zeros((128, 128), np.float32)
    for h in range(2):
        for l in range(108):
            fold[l, 64 * h + core_id[4 * h, l]] = 1.0
    spot = np.arange(40)
    wide = np.zeros((40, 128))
    consts = np.concatenate(
        [
            wide + (spot // 6)[:, None],
            wide + (spot % 6)[:, None],
            3 * half,
            offset_id,
        ]
    ).astype(np.float32)
    gather = np.concatenate([fold, fold])
    spread = np.concatenate([fold.T, fold.T])
    return consts, gather, spread


def determinant(m):
    return (
        m[0] * (m[4] * m[8] - m[5] * m[7])
        - m[1] * (m[3] * m[8] - m[5] * m[6])
        + m[2] * (m[3] * m[7] - m[4] * m[6])
    )


def low_part(x):
    return x - x.astype(jnp.bfloat16).astype(jnp.float32)


def high_low(x, axis):
    return jnp.concatenate([x, low_part(x)], axis=axis).astype(jnp.bfloat16)


def dot_nt(a, b):
    return lax.dot_general(a, b, (((1,), (1,)), ((), ())), preferred_element_type=jnp.float32)


def dot_nn(a, b):
    return lax.dot_general(a, b, (((1,), (0,)), ((), ())), preferred_element_type=jnp.float32)


def weight(node, spots):
    cell, _, first, second, third = spots
    shift = node - cell
    value = jnp.where(shift == 2.0, third, 0.0)
    value = jnp.where(shift == 1.0, second, value)
    return jnp.where(shift == 0.0, first, value)


def pair(ref, b):
    both = ref[pl.ds(pl.multiple_of(16 * b, 16), 16), :]
    return jnp.concatenate([both[0:8], both[8:16]], axis=1)


def partner(me, group, length):
    by = group + 1 if group < HOPS else -(group - HOPS + 1)
    return lax.rem(me + (by + length), length)


def step_kernel(
    length,
    links,
    rows,
    cells,
    offset_in,
    velocity_in,
    affine_in,
    strain_in,
    plastic_in,
    mass_in,
    live_in,
    consts,
    gather_mat,
    spread_mat,
    offset_out,
    velocity_out,
    affine_out,
    deform_out,
    plastic_out,
    move,
    affine8,
    deform8,
    ninth,
    plastic,
    elastic,
    part_a,
    part_b,
    part_c,
    part_d,
    spots_a,
    spots_b,
    weight_hi,
    weight_lo,
    first_w,
    first_d,
    own,
    table,
    leaving,
    speed,
    speed_side,
    speed_out,
    speed_in,
    padded,
    field,
    found_a,
    found_b,
    send_sem,
    recv_sem,
):
    me = lax.axis_index("dom")
    barrier = pltpu.get_barrier_semaphore()
    for g in range(GROUPS):
        pl.semaphore_signal(
            barrier,
            inc=1,
            device_id=(partner(me, g, length),),
            device_id_type=pl.DeviceIdType.MESH,
        )

    def partial_copy(step, g):
        return pltpu.make_async_remote_copy(
            src_ref=leaving.at[pl.ds(SLOTS * g, SLOTS)],
            dst_ref=table.at[pl.ds(OWN + SLOTS * g, SLOTS)],
            send_sem=send_sem.at[step, 0, g],
            recv_sem=recv_sem.at[step, 0, g],
            device_id=(partner(me, g, length),),
            device_id_type=pl.DeviceIdType.MESH,
        )

    def speed_copy(step, g):
        return pltpu.make_async_remote_copy(
            src_ref=speed_out.at[pl.ds(3 * g, 3)],
            dst_ref=speed_in.at[pl.ds(3 * g, 3)],
            send_sem=send_sem.at[step, 1, g],
            recv_sem=recv_sem.at[step, 1, g],
            device_id=(partner(me, g, length),),
            device_id_type=pl.DeviceIdType.MESH,
        )

    row_id = lax.broadcasted_iota(jnp.int32, (8, 128), 0)
    lane_id = lax.broadcasted_iota(jnp.int32, (8, 128), 1)
    upper = row_id < 4
    left = lane_id < 64
    diagonal = upper == left
    upper_left = upper & left
    lower_right = diagonal & ~upper
    channel = row_id % 4
    zero_tile = jnp.zeros((8, 128), jnp.float32)

    ones = jnp.where((row_id == 0) | (row_id == 4), 1.0, 0.0)

    def load_tile(t, carry):
        lanes = pl.ds(pl.multiple_of(128 * t, 128), 128)
        spot = pl.ds(pl.multiple_of(8 * t, 8), 8)
        move[spot, :] = jnp.concatenate(
            [offset_in[:, lanes], velocity_in[:, lanes], zero_tile[0:2]], axis=0
        )
        affine8[spot, :] = affine_in[0:8, lanes]
        deform8[spot, :] = strain_in[0:8, lanes] + ones
        ninth[spot, :] = jnp.concatenate(
            [affine_in[8:9, lanes], strain_in[8:9, lanes] + 1.0, zero_tile[0:6]], axis=0
        )
        part_b[spot, :] = zero_tile
        part_c[spot, :] = zero_tile
        part_d[spot, :] = zero_tile
        spots_b[spot, :] = zero_tile
        return carry

    lax.fori_loop(0, TILES, load_tile, 0, unroll=4)
    plastic[...] = plastic_in[...]
    table[NONE] = zero_tile
    padded[NONE] = zero_tile

    def one_step(step, carry):
        def particles(r, carry):
            band = pl.ds(pl.multiple_of(8 * r, 8), 8)

            def every(i):
                return pl.ds(64 * r + i, 8, stride=8)

            f = [deform8[every(k), :] for k in range(8)] + [ninth[every(1), :]]
            volume = determinant(f)
            clamped = jnp.clip(volume, 1.0 - COMPRESS, 1.0 + STRETCH)
            hardened = plastic[band, :] * volume / clamped
            factor = jnp.exp(jnp.log(clamped / volume) / 3.0)
            e = [x * factor for x in f]
            for k in range(9):
                elastic[k, band, :] = e[k]
            elastic[9, band, :] = hardened
            live = live_in[band, :] != 0
            mass = jnp.where(live, mass_in[band, :], 0.0)
            stiff = jnp.exp(HARDEN * (1.0 - hardened))
            shear = SHEAR * stiff
            bulk = BULK * stiff * jnp.log(clamped)
            part_a[every(0), :] = mass
            part_a[every(4), :] = mass
            for i in range(3):
                value = mass * move[every(3 + i), :]
                part_a[every(1 + i), :] = value
                part_a[every(5 + i), :] = value
            inner = {}
            for i in range(3):
                for j in range(i, 3):
                    total = (
                        e[3 * i] * e[3 * j]
                        + e[3 * i + 1] * e[3 * j + 1]
                        + e[3 * i + 2] * e[3 * j + 2]
                    )
                    stress = shear * (total - 1.0) + bulk if i == j else shear * total
                    inner[i, j] = inner[j, i] = stress
            for i in range(3):
                for j, target in enumerate((part_b, part_c, part_d)):
                    k = 3 * i + j
                    affine = affine8[every(k), :] if k < 8 else ninth[every(0), :]
                    value = mass * (affine - (4.0 * DT) * inner[i, j])
                    value = jnp.where(live, value, 0.0)
                    target[every(1 + i), :] = value
                    target[every(5 + i), :] = value
            cell = cells[band, :]
            corner = (cell >> 4, (cell >> 2) & 3, cell & 3)
            spots = []
            for i in range(3):
                c = corner[i].astype(jnp.float32)
                frac = 0.5 + move[every(i), :]
                spots += [
                    c,
                    c + frac,
                    0.5 * (1.5 - frac) * (1.5 - frac),
                    0.75 - (frac - 1.0) * (frac - 1.0),
                    0.5 * (frac - 0.5) * (frac - 0.5),
                ]
            for k, value in enumerate(spots):
                if k < 8:
                    spots_a[every(k), :] = value
                else:
                    spots_b[every(k - 8), :] = value
            return carry

        lax.fori_loop(0, TILES // 8, particles, 0)

        def scatter(b, carry):
            mass_flow = pair(part_a, b)
            push = [pair(part_b, b), pair(part_c, b), pair(part_d, b)]
            tile_a = pair(spots_a, b)
            tile_b = pair(spots_b, b)
            lines = [tile_a[k : k + 1] for k in range(8)] + [tile_b[k : k + 1] for k in range(7)]
            first, second, third = lines[0:5], lines[5:10], lines[10:15]
            base = consts[80:88, :]
            base = jnp.concatenate([base, base], axis=1)
            blocks = [[], [], []]
            weights = []
            for a in range(3):
                node = base + float(a)
                w = weight(node, first)
                d = w * (node - first[1])
                weights.append((w, d))
                blocks[0].append(w * mass_flow + d * push[0])
                blocks[1].append(w * push[1])
                blocks[2].append(w * push[2])
            spot = pl.ds(pl.multiple_of(24 * b, 8), 24)
            first_w[spot, :] = jnp.concatenate([w for w, d in weights], axis=0)
            first_d[spot, :] = jnp.concatenate([d for w, d in weights], axis=0)
            lhs = jnp.concatenate([jnp.concatenate(x, axis=0) for x in blocks], axis=1)
            node2 = consts[0:40, :]
            node2 = jnp.concatenate([node2, node2], axis=1)
            node3 = consts[40:80, :]
            node3 = jnp.concatenate([node3, node3], axis=1)
            w23 = weight(node2, second) * weight(node3, third)
            rhs = jnp.concatenate(
                [w23, w23 * (node2 - second[1]), w23 * (node3 - third[1])], axis=1
            )
            rhs = jnp.concatenate([rhs, jnp.zeros((8, 3 * PMAX), jnp.float32)], axis=0)
            high = rhs.astype(jnp.bfloat16)
            low = low_part(rhs).astype(jnp.bfloat16)
            spot = pl.ds(pl.multiple_of(48 * b, 16), 48)
            weight_hi[spot, :] = high
            weight_lo[spot, :] = low
            lhs = high_low(lhs, 0)
            both = dot_nt(lhs, high) + dot_nt(lhs, low)
            total = both[0:24] + both[24:48]
            block = jnp.concatenate(
                [total[0:8, 0:36], total[8:16, 0:36], total[16:24, 0:36], zero_tile[:, 0:20]],
                axis=1,
            )
            own[b] = block
            table[b] = block
            return carry

        lax.fori_loop(0, OWN, scatter, 0, unroll=2)

        @pl.when(step == 0)
        def _():
            pl.semaphore_wait(barrier, GROUPS)

        for g in range(GROUPS):
            for k in range(SLOTS):
                leaving[SLOTS * g + k] = own[rows[SLOTS * g + k]]
            partial_copy(step, g).start()
        for g in range(GROUPS):
            partial_copy(step, g).wait()

        offset_id = consts[88:96, :]

        def collect(o, total):
            here = offset_id == o.astype(jnp.float32)
            return tuple(
                jnp.where(here, table[links[OWN * o + b]], total[b]) for b in range(OWN)
            )

        total = lax.fori_loop(0, 27, collect, (zero_tile,) * OWN)
        total = dot_nn(high_low(jnp.concatenate(total, axis=0), 1), gather_mat[...])
        for b in range(OWN):
            node = total[8 * b : 8 * b + 8]
            node = node + pltpu.roll(pltpu.roll(node, 4, 0), 64, 1)
            node = jnp.where(diagonal, node, 0.0)
            mass = jnp.where(channel == 0, node, 0.0)
            mass = mass + pltpu.roll(mass, 1, 0)
            mass = mass + pltpu.roll(mass, 2, 0)
            node = node / jnp.maximum(mass, MASS_FLOOR)
            node = node - jnp.where(channel == 3, DT * GRAVITY, 0.0)
            node = jnp.where(diagonal, node, 0.0)
            speed[b] = node
            speed_side[b] = pltpu.roll(node, 64, 1)

        for g in range(GROUPS):
            for m in range(3):
                r = [rows[SLOTS * g + 4 * m + k] for k in range(4)]
                speed_out[3 * g + m] = jnp.where(upper, speed[r[0]], speed[r[1]]) + jnp.where(
                    upper, speed_side[r[2]], speed_side[r[3]]
                )
            speed_copy(step, g).start()

        def spread(tiles):
            x = high_low(jnp.concatenate(tiles, axis=0), 1)
            return dot_nn(x, spread_mat[...]).reshape(len(tiles), 8, 128)

        padded[0:OWN] = spread([speed[b] for b in range(OWN)])
        for g in range(GROUPS):
            speed_copy(step, g).wait()
            tiles = []
            for m in range(3):
                z = speed_in[3 * g + m]
                zs = pltpu.roll(z, 4, 0)
                zl = pltpu.roll(z, 64, 1)
                zd = pltpu.roll(zs, 64, 1)
                tiles.append(jnp.where(upper_left, z, jnp.where(lower_right, zd, 0.0)))
                tiles.append(jnp.where(upper_left, zd, jnp.where(lower_right, z, 0.0)))
                tiles.append(jnp.where(upper_left, zl, jnp.where(lower_right, zs, 0.0)))
                tiles.append(jnp.where(upper_left, zs, jnp.where(lower_right, zl, 0.0)))
            padded[OWN + SLOTS * g : OWN + SLOTS * g + SLOTS] = spread(tiles)

        def fetch(o, total):
            here = offset_id == (26 - o).astype(jnp.float32)
            return tuple(
                jnp.where(here, padded[links[OWN * o + b]], total[b]) for b in range(OWN)
            )

        total = lax.fori_loop(0, 27, fetch, (zero_tile,) * OWN)
        for b in range(OWN):
            field[b] = total[b]

        upper_wide = lax.broadcasted_iota(jnp.int32, (8, PMAX), 0) < 4

        def gather(b, carry):
            v = field[b]
            v = jnp.concatenate([v[:, 0:48], v[:, 36:84], v[:, 72:120]], axis=0)
            v = high_low(v, 0)
            spot = pl.ds(pl.multiple_of(48 * b, 16), 48)
            both = dot_nn(v, weight_hi[spot, :]) + dot_nn(v, weight_lo[spot, :])
            result = both[0:24] + both[24:48]
            spot = pl.ds(pl.multiple_of(24 * b, 8), 24)

            def fold(x):
                x = x[0:8] + x[8:16] + x[16:24]
                return x + pltpu.roll(x, 4, 0)

            w = first_w[spot, :]
            plain = fold(w * result[:, 0:PMAX])
            by1 = fold(first_d[spot, :] * result[:, 0:PMAX])
            by2 = fold(w * result[:, PMAX : 2 * PMAX])
            by3 = fold(w * result[:, 2 * PMAX : 3 * PMAX])
            spot = pl.ds(pl.multiple_of(16 * b, 16), 16)
            out = jnp.where(upper_wide, plain, by1)
            found_a[spot, :] = jnp.concatenate([out[:, 0:128], out[:, 128:256]], axis=0)
            out = jnp.where(upper_wide, by2, by3)
            found_b[spot, :] = jnp.concatenate([out[:, 0:128], out[:, 128:256]], axis=0)
            return carry

        lax.fori_loop(0, OWN, gather, 0, unroll=2)

        def finish(r, carry):
            band = pl.ds(pl.multiple_of(8 * r, 8), 8)

            def every(i):
                return pl.ds(64 * r + i, 8, stride=8)

            live = live_in[band, :] != 0

            def put(ref, i, value):
                ref[every(i), :] = jnp.where(live, value, ref[every(i), :])

            v = [found_a[every(1 + i), :] for i in range(3)]
            moment = [
                [found_a[every(5 + i), :] for i in range(3)],
                [found_b[every(1 + i), :] for i in range(3)],
                [found_b[every(5 + i), :] for i in range(3)],
            ]
            affine = [4.0 * moment[j][i] for i in range(3) for j in range(3)]
            e = [elastic[k, band, :] for k in range(9)]
            for i in range(3):
                put(move, i, move[every(i), :] + DT * v[i])
                put(move, 3 + i, v[i])
            for i in range(3):
                for j in range(3):
                    k = 3 * i + j
                    total = e[k]
                    for m in range(3):
                        total = total + DT * affine[3 * i + m] * e[3 * m + j]
                    if k < 8:
                        put(affine8, k, affine[k])
                        put(deform8, k, total)
                    else:
                        put(ninth, 0, affine[k])
                        put(ninth, 1, total)
            plastic[band, :] = jnp.where(live, elastic[9, band, :], plastic[band, :])
            return carry

        lax.fori_loop(0, TILES // 8, finish, 0)
        return carry

    lax.fori_loop(0, 2, one_step, 0)

    def store_tile(t, carry):
        lanes = pl.ds(pl.multiple_of(128 * t, 128), 128)
        spot = pl.ds(pl.multiple_of(8 * t, 8), 8)
        value = move[spot, :]
        offset_out[:, lanes] = value[0:3]
        velocity_out[:, lanes] = value[3:6]
        affine_out[0:8, lanes] = affine8[spot, :]
        deform_out[0:8, lanes] = deform8[spot, :]
        value = ninth[spot, :]
        affine_out[8:9, lanes] = value[0:1]
        deform_out[8:9, lanes] = value[1:2]
        return carry

    lax.fori_loop(0, TILES, store_tile, 0, unroll=4)
    plastic_out[...] = plastic[...]


def on_device(
    length,
    base_cell,
    offset,
    velocity,
    affine,
    strain,
    plastic,
    particle_mass,
    counts,
    neighbours,
    send_rows,
):
    me = lax.axis_index("dom")
    remote = jnp.maximum(neighbours - OWN, 0)
    group = remote // SLOTS
    source = jnp.where(group < HOPS, me - (group + 1), me + (group - HOPS + 1))
    present = (neighbours >= 0) & ((neighbours < OWN) | ((source >= 0) & (source < length)))
    links = jnp.where(present, neighbours, NONE).T.reshape(-1)
    slot = jnp.arange(PMAX, dtype=jnp.int32)[None, :]
    live = (slot < counts[:, None]).astype(jnp.int32).reshape(TILES, 128)
    consts, gather_mat, spread_mat = tables()
    vmem = pl.BlockSpec(memory_space=pltpu.VMEM)
    smem = pl.BlockSpec(memory_space=pltpu.SMEM)
    f32 = jnp.float32
    tile = pltpu.VMEM((8 * TILES, 128), f32)
    planar = (TILES, 128)
    outs = pl.pallas_call(
        lambda *refs: step_kernel(length, *refs),
        out_shape=(
            jax.ShapeDtypeStruct((3, PARTICLES), f32),
            jax.ShapeDtypeStruct((3, PARTICLES), f32),
            jax.ShapeDtypeStruct((9, PARTICLES), f32),
            jax.ShapeDtypeStruct((9, PARTICLES), f32),
            jax.ShapeDtypeStruct(planar, f32),
        ),
        in_specs=[smem, smem] + [vmem] * 11,
        out_specs=(vmem,) * 5,
        scratch_shapes=[
            tile,
            tile,
            tile,
            tile,
            pltpu.VMEM(planar, f32),
            pltpu.VMEM((10,) + planar, f32),
            tile,
            tile,
            tile,
            tile,
            tile,
            tile,
            pltpu.VMEM((48 * OWN, 3 * PMAX), jnp.bfloat16),
            pltpu.VMEM((48 * OWN, 3 * PMAX), jnp.bfloat16),
            pltpu.VMEM((24 * OWN, PMAX), f32),
            pltpu.VMEM((24 * OWN, PMAX), f32),
            pltpu.VMEM((OWN, 8, 128), f32),
            pltpu.VMEM((NONE + 1, 8, 128), f32),
            pltpu.VMEM((RECEIVED, 8, 128), f32),
            pltpu.VMEM((OWN, 8, 128), f32),
            pltpu.VMEM((OWN, 8, 128), f32),
            pltpu.VMEM((3 * GROUPS, 8, 128), f32),
            pltpu.VMEM((3 * GROUPS, 8, 128), f32),
            pltpu.VMEM((NONE + 1, 8, 128), f32),
            pltpu.VMEM((OWN, 8, 128), f32),
            tile,
            tile,
            pltpu.SemaphoreType.DMA((2, 2, GROUPS)),
            pltpu.SemaphoreType.DMA((2, 2, GROUPS)),
        ],
        compiler_params=pltpu.CompilerParams(
            collective_id=0, has_side_effects=True, vmem_limit_bytes=40 * 1024 * 1024
        ),
        name="snow_steps",
    )(
        links,
        send_rows.reshape(-1),
        base_cell.reshape(planar),
        offset,
        velocity,
        affine,
        strain,
        plastic.reshape(planar),
        particle_mass.reshape(planar),
        live,
        jnp.asarray(consts),
        jnp.asarray(gather_mat, dtype=jnp.bfloat16),
        jnp.asarray(spread_mat, dtype=jnp.bfloat16),
    )
    return outs[:4] + (outs[4].reshape(PARTICLES),)


def solution(mesh):
    length = mesh.shape["dom"]
    wide = P(None, "dom")
    flat = P("dom")
    return jax.shard_map(
        lambda *args: on_device(length, *args),
        mesh=mesh,
        in_specs=(flat, wide, wide, wide, wide, flat, flat, flat, P("dom", None), P("dom", None)),
        out_specs=(wide, wide, wide, wide, flat),
        check_vma=False,
    )
```

```python
import jax
import jax.numpy as jnp
import numpy as np
from jax import lax
from jax.experimental import pallas as pl
from jax.experimental.pallas import tpu as pltpu
from jax.sharding import PartitionSpec as P

OWN = 16
PMAX = 256
HOPS = 4
SLOTS = 12
GROUPS = 2 * HOPS
RECEIVED = GROUPS * SLOTS
TABLE = 1 + OWN + RECEIVED
PARTICLES = OWN * PMAX
TILES = PARTICLES // 128

DT = 0.05
SHEAR = 4.0
BULK = 4.0
HARDEN = 10.0
COMPRESS = 0.025
STRETCH = 0.0075
GRAVITY = 1.0
MASS_FLOOR = 0.25


def tables():
    row = np.arange(8)[:, None]
    lane = np.arange(128)[None, :]
    half = row // 4 + 0 * lane
    third = lane // 36 + 0 * row
    place = lane % 36 + 0 * row
    inside = third < 3
    node = [3 * half + third, place // 6, place % 6]
    step = [(x == 0).astype(int) - (x == 5).astype(int) for x in node]
    offset_id = 9 * (step[0] + 1) + 3 * (step[1] + 1) + step[2] + 1
    offset_id = np.where(inside, offset_id, 13)
    core = [(x + 3) % 4 for x in node]
    core_id = np.where(inside, 16 * core[0] + 4 * core[1] + core[2], -1)
    fold = np.zeros((128, 128), np.float32)
    for h in range(2):
        for l in range(108):
            fold[l, 64 * h + core_id[4 * h, l]] = 1.0
    spot = np.arange(40)
    wide = np.zeros((40, 128))
    consts = np.concatenate(
        [
            wide + (spot // 6)[:, None],
            wide + (spot % 6)[:, None],
            3 * half,
            offset_id,
        ]
    ).astype(np.float32)
    folds = np.stack([np.concatenate([fold, fold]), np.concatenate([fold.T, fold.T])])
    return consts, folds


def determinant(m):
    return (
        m[0] * (m[4] * m[8] - m[5] * m[7])
        - m[1] * (m[3] * m[8] - m[5] * m[6])
        + m[2] * (m[3] * m[7] - m[4] * m[6])
    )


def low_part(x):
    return x - x.astype(jnp.bfloat16).astype(jnp.float32)


def high_low(x, axis):
    return jnp.concatenate([x, low_part(x)], axis=axis).astype(jnp.bfloat16)


def dot_nt(a, b):
    return lax.dot_general(a, b, (((1,), (1,)), ((), ())), preferred_element_type=jnp.float32)


def dot_nn(a, b):
    return lax.dot_general(a, b, (((1,), (0,)), ((), ())), preferred_element_type=jnp.float32)


def weight(node, spots):
    cell, _, first, second, third = spots
    shift = node - cell
    value = jnp.where(shift == 2.0, third, 0.0)
    value = jnp.where(shift == 1.0, second, value)
    return jnp.where(shift == 0.0, first, value)


def pair(ref, b):
    both = ref[pl.ds(pl.multiple_of(16 * b, 16), 16), :]
    return jnp.concatenate([both[0:8], both[8:16]], axis=1)


def partner(me, group, length):
    by = group + 1 if group < HOPS else -(group - HOPS + 1)
    return lax.rem(me + (by + length), length)


def step_kernel(length, *refs):
    given, results, held, work = refs[0:12], refs[12:17], refs[17:29], refs[29:]
    (
        links,
        rows,
        counts,
        cells,
        offset_in,
        velocity_in,
        affine_in,
        strain_in,
        plastic_in,
        mass_in,
        consts,
        fold_mats,
    ) = held
    offset_out, velocity_out, affine_out, deform_out, plastic = results
    (
        move,
        affine8,
        deform8,
        ninth,
        elastic,
        part_a,
        part_b,
        part_c,
        part_d,
        spots_a,
        spots_b,
        weight_hi,
        weight_lo,
        first_w,
        first_d,
        own,
        table,
        leaving,
        speed,
        speed_side,
        speed_out,
        speed_in,
        padded,
        field,
        found_a,
        found_b,
        send_sem,
        recv_sem,
        load_sem,
    ) = work
    loads = [pltpu.make_async_copy(given[k], held[k], load_sem.at[k]) for k in range(12)]
    for copy in loads:
        copy.start()
    me = lax.axis_index("dom")
    barrier = pltpu.get_barrier_semaphore()
    for g in range(GROUPS):
        pl.semaphore_signal(
            barrier,
            inc=1,
            device_id=(partner(me, g, length),),
            device_id_type=pl.DeviceIdType.MESH,
        )

    def partial_copy(step, g):
        return pltpu.make_async_remote_copy(
            src_ref=leaving.at[pl.ds(SLOTS * g, SLOTS)],
            dst_ref=table.at[pl.ds(1 + OWN + SLOTS * g, SLOTS)],
            send_sem=send_sem.at[step, 0, g],
            recv_sem=recv_sem.at[step, 0, g],
            device_id=(partner(me, g, length),),
            device_id_type=pl.DeviceIdType.MESH,
        )

    def speed_copy(step, g):
        return pltpu.make_async_remote_copy(
            src_ref=speed_out.at[pl.ds(3 * g, 3)],
            dst_ref=speed_in.at[pl.ds(3 * g, 3)],
            send_sem=send_sem.at[step, 1, g],
            recv_sem=recv_sem.at[step, 1, g],
            device_id=(partner(me, g, length),),
            device_id_type=pl.DeviceIdType.MESH,
        )

    def drop_outside(ref, g):
        source = me - (g + 1) if g < HOPS else me + (g - HOPS + 1)

        @pl.when((source < 0) | (source >= length))
        def _():
            ref[1 + OWN + SLOTS * g : 1 + OWN + SLOTS * (g + 1)] = jnp.zeros(
                (SLOTS, 8, 128), jnp.float32
            )

    row_id = lax.broadcasted_iota(jnp.int32, (8, 128), 0)
    lane_id = lax.broadcasted_iota(jnp.int32, (8, 128), 1)
    upper = row_id < 4
    left = lane_id < 64
    diagonal = upper == left
    upper_left = upper & left
    lower_right = diagonal & ~upper
    channel = row_id % 4
    zero_tile = jnp.zeros((8, 128), jnp.float32)

    slot = lane_id + 128 * (row_id % 2)

    def live_slots(r):
        limit = counts[4 * r + 3]
        for k in (2, 1, 0):
            limit = jnp.where(row_id < 2 * k + 2, counts[4 * r + k], limit)
        return slot < limit

    ones = jnp.where((row_id == 0) | (row_id == 4), 1.0, 0.0)

    def load_tile(t, carry):
        lanes = pl.ds(pl.multiple_of(128 * t, 128), 128)
        spot = pl.ds(pl.multiple_of(8 * t, 8), 8)
        move[spot, :] = jnp.concatenate(
            [offset_in[:, lanes], velocity_in[:, lanes], zero_tile[0:2]], axis=0
        )
        affine8[spot, :] = affine_in[0:8, lanes]
        deform8[spot, :] = strain_in[0:8, lanes] + ones
        ninth[spot, :] = jnp.concatenate(
            [affine_in[8:9, lanes], strain_in[8:9, lanes] + 1.0, zero_tile[0:6]], axis=0
        )
        part_b[spot, :] = zero_tile
        part_c[spot, :] = zero_tile
        part_d[spot, :] = zero_tile
        spots_b[spot, :] = zero_tile
        return carry

    for copy in loads:
        copy.wait()
    lax.fori_loop(0, TILES, load_tile, 0, unroll=4)
    plastic[...] = plastic_in[...]
    table[0] = zero_tile
    padded[0] = zero_tile

    def one_step(step, carry):
        def particles(r, carry):
            band = pl.ds(pl.multiple_of(8 * r, 8), 8)

            def every(i):
                return pl.ds(64 * r + i, 8, stride=8)

            f = [deform8[every(k), :] for k in range(8)] + [ninth[every(1), :]]
            volume = determinant(f)
            clamped = jnp.clip(volume, 1.0 - COMPRESS, 1.0 + STRETCH)
            hardened = plastic[band, :] * volume / clamped
            factor = jnp.exp(jnp.log(clamped / volume) / 3.0)
            e = [x * factor for x in f]
            for k in range(9):
                elastic[k, band, :] = e[k]
            elastic[9, band, :] = hardened
            live = live_slots(r)
            mass = jnp.where(live, mass_in[band, :], 0.0)
            stiff = jnp.exp(HARDEN * (1.0 - hardened))
            shear = SHEAR * stiff
            bulk = BULK * stiff * jnp.log(clamped)
            part_a[every(0), :] = mass
            part_a[every(4), :] = mass
            for i in range(3):
                value = mass * move[every(3 + i), :]
                part_a[every(1 + i), :] = value
                part_a[every(5 + i), :] = value
            inner = {}
            for i in range(3):
                for j in range(i, 3):
                    total = (
                        e[3 * i] * e[3 * j]
                        + e[3 * i + 1] * e[3 * j + 1]
                        + e[3 * i + 2] * e[3 * j + 2]
                    )
                    stress = shear * (total - 1.0) + bulk if i == j else shear * total
                    inner[i, j] = inner[j, i] = stress
            for i in range(3):
                for j, target in enumerate((part_b, part_c, part_d)):
                    k = 3 * i + j
                    affine = affine8[every(k), :] if k < 8 else ninth[every(0), :]
                    value = mass * (affine - (4.0 * DT) * inner[i, j])
                    value = jnp.where(live, value, 0.0)
                    target[every(1 + i), :] = value
                    target[every(5 + i), :] = value
            cell = cells[band, :]
            corner = (cell >> 4, (cell >> 2) & 3, cell & 3)
            spots = []
            for i in range(3):
                c = corner[i].astype(jnp.float32)
                frac = 0.5 + move[every(i), :]
                spots += [
                    c,
                    c + frac,
                    0.5 * (1.5 - frac) * (1.5 - frac),
                    0.75 - (frac - 1.0) * (frac - 1.0),
                    0.5 * (frac - 0.5) * (frac - 0.5),
                ]
            for k, value in enumerate(spots):
                if k < 8:
                    spots_a[every(k), :] = value
                else:
                    spots_b[every(k - 8), :] = value
            return carry

        lax.fori_loop(0, TILES // 8, particles, 0)

        def scatter(b, carry):
            mass_flow = pair(part_a, b)
            push = [pair(part_b, b), pair(part_c, b), pair(part_d, b)]
            tile_a = pair(spots_a, b)
            tile_b = pair(spots_b, b)
            lines = [tile_a[k : k + 1] for k in range(8)] + [tile_b[k : k + 1] for k in range(7)]
            first, second, third = lines[0:5], lines[5:10], lines[10:15]
            base = consts[80:88, :]
            base = jnp.concatenate([base, base], axis=1)
            blocks = [[], [], []]
            weights = []
            for a in range(3):
                node = base + float(a)
                w = weight(node, first)
                d = w * (node - first[1])
                weights.append((w, d))
                blocks[0].append(w * mass_flow + d * push[0])
                blocks[1].append(w * push[1])
                blocks[2].append(w * push[2])
            spot = pl.ds(pl.multiple_of(24 * b, 8), 24)
            first_w[spot, :] = jnp.concatenate([w for w, d in weights], axis=0)
            first_d[spot, :] = jnp.concatenate([d for w, d in weights], axis=0)
            lhs = jnp.concatenate([jnp.concatenate(x, axis=0) for x in blocks], axis=1)
            node2 = consts[0:40, :]
            node2 = jnp.concatenate([node2, node2], axis=1)
            node3 = consts[40:80, :]
            node3 = jnp.concatenate([node3, node3], axis=1)
            w23 = weight(node2, second) * weight(node3, third)
            rhs = jnp.concatenate(
                [w23, w23 * (node2 - second[1]), w23 * (node3 - third[1])], axis=1
            )
            rhs = jnp.concatenate([rhs, jnp.zeros((8, 3 * PMAX), jnp.float32)], axis=0)
            high = rhs.astype(jnp.bfloat16)
            low = low_part(rhs).astype(jnp.bfloat16)
            spot = pl.ds(pl.multiple_of(48 * b, 16), 48)
            weight_hi[spot, :] = high
            weight_lo[spot, :] = low
            lhs = high_low(lhs, 0)
            both = dot_nt(lhs, high) + dot_nt(lhs, low)
            total = both[0:24] + both[24:48]
            block = jnp.concatenate(
                [total[0:8, 0:36], total[8:16, 0:36], total[16:24, 0:36], zero_tile[:, 0:20]],
                axis=1,
            )
            own[b] = block
            table[1 + b] = block
            return carry

        lax.fori_loop(0, OWN, scatter, 0, unroll=8)

        @pl.when(step == 0)
        def _():
            pl.semaphore_wait(barrier, GROUPS)

        for g in range(GROUPS):
            for k in range(SLOTS):
                leaving[SLOTS * g + k] = own[rows[0, SLOTS * g + k]]
            partial_copy(step, g).start()
        for g in range(GROUPS):
            partial_copy(step, g).wait()
            drop_outside(table, g)

        offset_id = consts[88:96, :]

        def collect(o, total):
            here = offset_id == o.astype(jnp.float32)
            return tuple(
                jnp.where(here, table[1 + links[b, o]], total[b]) for b in range(OWN)
            )

        total = lax.fori_loop(0, 27, collect, (zero_tile,) * OWN)
        total = dot_nn(high_low(jnp.concatenate(total, axis=0), 1), fold_mats[0])
        for b in range(OWN):
            node = total[8 * b : 8 * b + 8]
            node = node + pltpu.roll(pltpu.roll(node, 4, 0), 64, 1)
            node = jnp.where(diagonal, node, 0.0)
            mass = jnp.where(channel == 0, node, 0.0)
            mass = mass + pltpu.roll(mass, 1, 0)
            mass = mass + pltpu.roll(mass, 2, 0)
            node = node / jnp.maximum(mass, MASS_FLOOR)
            node = node - jnp.where(channel == 3, DT * GRAVITY, 0.0)
            node = jnp.where(diagonal, node, 0.0)
            speed[b] = node
            speed_side[b] = pltpu.roll(node, 64, 1)

        for g in range(GROUPS):
            for m in range(3):
                r = [rows[0, SLOTS * g + 4 * m + k] for k in range(4)]
                speed_out[3 * g + m] = jnp.where(upper, speed[r[0]], speed[r[1]]) + jnp.where(
                    upper, speed_side[r[2]], speed_side[r[3]]
                )
            speed_copy(step, g).start()

        def spread(tiles):
            x = high_low(jnp.concatenate(tiles, axis=0), 1)
            return dot_nn(x, fold_mats[1]).reshape(len(tiles), 8, 128)

        padded[1 : 1 + OWN] = spread([speed[b] for b in range(OWN)])
        for g in range(GROUPS):
            speed_copy(step, g).wait()
            tiles = []
            for m in range(3):
                z = speed_in[3 * g + m]
                zs = pltpu.roll(z, 4, 0)
                zl = pltpu.roll(z, 64, 1)
                zd = pltpu.roll(zs, 64, 1)
                tiles.append(jnp.where(upper_left, z, jnp.where(lower_right, zd, 0.0)))
                tiles.append(jnp.where(upper_left, zd, jnp.where(lower_right, z, 0.0)))
                tiles.append(jnp.where(upper_left, zl, jnp.where(lower_right, zs, 0.0)))
                tiles.append(jnp.where(upper_left, zs, jnp.where(lower_right, zl, 0.0)))
            padded[1 + OWN + SLOTS * g : 1 + OWN + SLOTS * (g + 1)] = spread(tiles)
            drop_outside(padded, g)

        def fetch(o, total):
            here = offset_id == (26 - o).astype(jnp.float32)
            return tuple(
                jnp.where(here, padded[1 + links[b, o]], total[b]) for b in range(OWN)
            )

        total = lax.fori_loop(0, 27, fetch, (zero_tile,) * OWN)
        for b in range(OWN):
            field[b] = total[b]

        upper_wide = lax.broadcasted_iota(jnp.int32, (8, PMAX), 0) < 4

        def gather(b, carry):
            v = field[b]
            v = jnp.concatenate([v[:, 0:48], v[:, 36:84], v[:, 72:120]], axis=0)
            v = high_low(v, 0)
            spot = pl.ds(pl.multiple_of(48 * b, 16), 48)
            both = dot_nn(v, weight_hi[spot, :]) + dot_nn(v, weight_lo[spot, :])
            result = both[0:24] + both[24:48]
            spot = pl.ds(pl.multiple_of(24 * b, 8), 24)

            def fold(x):
                x = x[0:8] + x[8:16] + x[16:24]
                return x + pltpu.roll(x, 4, 0)

            w = first_w[spot, :]
            plain = fold(w * result[:, 0:PMAX])
            by1 = fold(first_d[spot, :] * result[:, 0:PMAX])
            by2 = fold(w * result[:, PMAX : 2 * PMAX])
            by3 = fold(w * result[:, 2 * PMAX : 3 * PMAX])
            spot = pl.ds(pl.multiple_of(16 * b, 16), 16)
            out = jnp.where(upper_wide, plain, by1)
            found_a[spot, :] = jnp.concatenate([out[:, 0:128], out[:, 128:256]], axis=0)
            out = jnp.where(upper_wide, by2, by3)
            found_b[spot, :] = jnp.concatenate([out[:, 0:128], out[:, 128:256]], axis=0)
            return carry

        lax.fori_loop(0, OWN, gather, 0, unroll=8)

        def finish(r, carry):
            band = pl.ds(pl.multiple_of(8 * r, 8), 8)

            def every(i):
                return pl.ds(64 * r + i, 8, stride=8)

            live = live_slots(r)

            def put(ref, i, value):
                ref[every(i), :] = jnp.where(live, value, ref[every(i), :])

            v = [found_a[every(1 + i), :] for i in range(3)]
            moment = [
                [found_a[every(5 + i), :] for i in range(3)],
                [found_b[every(1 + i), :] for i in range(3)],
                [found_b[every(5 + i), :] for i in range(3)],
            ]
            affine = [4.0 * moment[j][i] for i in range(3) for j in range(3)]
            e = [elastic[k, band, :] for k in range(9)]
            for i in range(3):
                put(move, i, move[every(i), :] + DT * v[i])
                put(move, 3 + i, v[i])
            for i in range(3):
                for j in range(3):
                    k = 3 * i + j
                    total = e[k]
                    for m in range(3):
                        total = total + DT * affine[3 * i + m] * e[3 * m + j]
                    if k < 8:
                        put(affine8, k, affine[k])
                        put(deform8, k, total)
                    else:
                        put(ninth, 0, affine[k])
                        put(ninth, 1, total)
            plastic[band, :] = jnp.where(live, elastic[9, band, :], plastic[band, :])
            return carry

        lax.fori_loop(0, TILES // 8, finish, 0)
        return carry

    lax.fori_loop(0, 2, one_step, 0)

    def store_tile(t, carry):
        lanes = pl.ds(pl.multiple_of(128 * t, 128), 128)
        spot = pl.ds(pl.multiple_of(8 * t, 8), 8)
        value = move[spot, :]
        offset_out[:, lanes] = value[0:3]
        velocity_out[:, lanes] = value[3:6]
        affine_out[0:8, lanes] = affine8[spot, :]
        deform_out[0:8, lanes] = deform8[spot, :]
        value = ninth[spot, :]
        affine_out[8:9, lanes] = value[0:1]
        deform_out[8:9, lanes] = value[1:2]
        return carry

    lax.fori_loop(0, TILES, store_tile, 0, unroll=4)


def hand_over(*refs):
    first, last, held = refs[0:5], refs[5:10], refs[10:15]
    copies = []
    for k in range(5):
        come = pltpu.make_async_copy(first[k], held[k], refs[15].at[0, k])
        leave = pltpu.make_async_copy(held[k], last[k], refs[15].at[1, k])
        copies.append((come, leave))
        come.start()
    for come, leave in copies:
        come.wait()
        leave.start()
    for come, leave in copies:
        leave.wait()


def on_device(
    length,
    base_cell,
    offset,
    velocity,
    affine,
    strain,
    plastic,
    particle_mass,
    counts,
    neighbours,
    send_rows,
):
    consts, folds = tables()
    hbm = pl.BlockSpec(memory_space=pltpu.HBM)
    vmem = pl.BlockSpec(memory_space=pltpu.VMEM)
    f32 = jnp.float32
    i32 = jnp.int32
    tile = pltpu.VMEM((8 * TILES, 128), f32)
    planar = (TILES, 128)
    row3 = (3, PARTICLES)
    row9 = (9, PARTICLES)
    shapes = [jax.ShapeDtypeStruct(x, f32) for x in (row3, row3, row9, row9, planar)]
    outs = pl.pallas_call(
        lambda *refs: step_kernel(length, *refs),
        out_shape=shapes,
        in_specs=[hbm] * 12,
        out_specs=[vmem] * 5,
        scratch_shapes=[
            pltpu.SMEM((OWN, 27), i32),
            pltpu.SMEM((1, RECEIVED), i32),
            pltpu.SMEM((OWN,), i32),
            pltpu.VMEM(planar, i32),
            pltpu.VMEM(row3, f32),
            pltpu.VMEM(row3, f32),
            pltpu.VMEM(row9, f32),
            pltpu.VMEM(row9, f32),
            pltpu.VMEM(planar, f32),
            pltpu.VMEM(planar, f32),
            pltpu.VMEM((96, 128), f32),
            pltpu.VMEM((2, 256, 128), jnp.bfloat16),
            tile,
            tile,
            tile,
            tile,
            pltpu.VMEM((10,) + planar, f32),
            tile,
            tile,
            tile,
            tile,
            tile,
            tile,
            pltpu.VMEM((48 * OWN, 3 * PMAX), jnp.bfloat16),
            pltpu.VMEM((48 * OWN, 3 * PMAX), jnp.bfloat16),
            pltpu.VMEM((24 * OWN, PMAX), f32),
            pltpu.VMEM((24 * OWN, PMAX), f32),
            pltpu.VMEM((OWN, 8, 128), f32),
            pltpu.VMEM((TABLE, 8, 128), f32),
            pltpu.VMEM((RECEIVED, 8, 128), f32),
            pltpu.VMEM((OWN, 8, 128), f32),
            pltpu.VMEM((OWN, 8, 128), f32),
            pltpu.VMEM((3 * GROUPS, 8, 128), f32),
            pltpu.VMEM((3 * GROUPS, 8, 128), f32),
            pltpu.VMEM((TABLE, 8, 128), f32),
            pltpu.VMEM((OWN, 8, 128), f32),
            tile,
            tile,
            pltpu.SemaphoreType.DMA((2, 2, GROUPS)),
            pltpu.SemaphoreType.DMA((2, 2, GROUPS)),
            pltpu.SemaphoreType.DMA((12,)),
        ],
        compiler_params=pltpu.CompilerParams(
            collective_id=0, has_side_effects=True, vmem_limit_bytes=62 * 1024 * 1024
        ),
        name="snow_steps",
    )(
        neighbours,
        send_rows,
        counts,
        base_cell.reshape(planar),
        offset,
        velocity,
        affine,
        strain,
        plastic.reshape(planar),
        particle_mass.reshape(planar),
        jnp.asarray(consts),
        jnp.asarray(folds, dtype=jnp.bfloat16),
    )
    outs = pl.pallas_call(
        hand_over,
        out_shape=shapes,
        in_specs=[hbm] * 5,
        out_specs=[hbm] * 5,
        scratch_shapes=[pltpu.VMEM(x.shape, f32) for x in shapes] + [pltpu.SemaphoreType.DMA((2, 5))],
        compiler_params=pltpu.CompilerParams(vmem_limit_bytes=62 * 1024 * 1024),
        name="hand_over",
    )(*outs)
    return tuple(outs[:4]) + (outs[4].reshape(PARTICLES),)


def solution(mesh):
    length = mesh.shape["dom"]
    wide = P(None, "dom")
    flat = P("dom")
    return jax.shard_map(
        lambda *args: on_device(length, *args),
        mesh=mesh,
        in_specs=(flat, wide, wide, wide, wide, flat, flat, flat, P("dom", None), P("dom", None)),
        out_specs=(wide, wide, wide, wide, flat),
        check_vma=False,
    )
```

```python
import jax
import jax.numpy as jnp
import numpy as np
from jax import lax
from jax.experimental import pallas as pl
from jax.experimental.pallas import tpu as pltpu
from jax.sharding import PartitionSpec as P

OWN = 16
PMAX = 256
HOPS = 4
SLOTS = 12
GROUPS = 2 * HOPS
RECEIVED = GROUPS * SLOTS
TABLE = 1 + OWN + RECEIVED
PARTICLES = OWN * PMAX
TILES = PARTICLES // 128
RIM = 20
USED = 36 + 2 * RIM
SENT = 8
FAR_FIRST = (3, 7, 2, 6, 1, 5, 0, 4)
NEAR_FIRST = (0, 4, 1, 5, 2, 6, 3, 7)

DT = 0.05
SHEAR = 4.0
BULK = 4.0
HARDEN = 10.0
COMPRESS = 0.025
STRETCH = 0.0075
GRAVITY = 1.0
MASS_FLOOR = 0.25


def tables():
    places = [(j2, j3) for j2 in range(6) for j3 in range(6)]
    places.sort(key=lambda x: (x[0] in (1, 2, 3, 4) and x[1] in (1, 2, 3, 4), x))
    lanes = [(0, q) for q in range(36)]
    lanes += [(a, q) for a in (1, 2) for q in range(RIM)]
    lanes += [(a, q) for a in (1, 2) for q in range(RIM, 36)]
    lanes += [(3, 0)] * 20
    half = np.arange(8)[:, None] // 4 + np.zeros((1, 128), int)
    third = np.array([x[0] for x in lanes])[None, :] + 0 * half
    place = np.array([x[1] for x in lanes])[None, :] + 0 * half
    inside = third < 3
    spot2 = np.array([x[0] for x in places])
    spot3 = np.array([x[1] for x in places])
    node = [np.where(half == 0, third, 5 - third), spot2[place], spot3[place]]
    step = [(x == 0).astype(int) - (x == 5).astype(int) for x in node]
    offset_id = 9 * (step[0] + 1) + 3 * (step[1] + 1) + step[2] + 1
    offset_id = np.where(inside, offset_id, 13)
    core = [(x + 3) % 4 for x in node]
    core_id = np.where(inside, 16 * core[0] + 4 * core[1] + core[2], -1)
    fold = np.zeros((128, 128), np.float32)
    for h in range(2):
        for l in range(108):
            fold[l, 64 * h + core_id[4 * h, l]] = 1.0
    wide = np.zeros((40, 128))
    none = [6] * 4
    consts = np.concatenate(
        [
            wide + np.append(spot2, none)[:, None],
            wide + np.append(spot3, none)[:, None],
            np.where(half == 0, 0, 5),
            np.where(half == 0, 1, 4),
            np.where(half == 0, 2, 3),
            offset_id,
        ]
    ).astype(np.float32)
    folds = np.stack([np.concatenate([fold, fold]), np.concatenate([fold.T, fold.T])])
    return consts, folds


def determinant(m):
    return (
        m[0] * (m[4] * m[8] - m[5] * m[7])
        - m[1] * (m[3] * m[8] - m[5] * m[6])
        + m[2] * (m[3] * m[7] - m[4] * m[6])
    )


def low_part(x):
    return x - x.astype(jnp.bfloat16).astype(jnp.float32)


def high_low(x, axis):
    return jnp.concatenate([x, low_part(x)], axis=axis).astype(jnp.bfloat16)


def dot_nt(a, b):
    return lax.dot_general(a, b, (((1,), (1,)), ((), ())), preferred_element_type=jnp.float32)


def dot_nn(a, b):
    return lax.dot_general(a, b, (((1,), (0,)), ((), ())), preferred_element_type=jnp.float32)


def weight(node, spots):
    cell, _, first, second, third = spots
    shift = node - cell
    value = jnp.where(shift == 2.0, third, 0.0)
    value = jnp.where(shift == 1.0, second, value)
    return jnp.where(shift == 0.0, first, value)


def pair(ref, b):
    both = ref[pl.ds(pl.multiple_of(16 * b, 16), 16), :]
    return jnp.concatenate([both[0:8], both[8:16]], axis=1)


def reach(group):
    return group + 1 if group < HOPS else -(group - HOPS + 1)


def partner(me, group, length):
    return lax.rem(me + (reach(group) + length), length)


def step_kernel(length, *refs):
    given, results, held, work = refs[0:12], refs[12:17], refs[17:29], refs[29:]
    (
        links,
        rows,
        counts,
        cells,
        offset_in,
        velocity_in,
        affine_in,
        strain_in,
        plastic_in,
        mass_in,
        consts,
        fold_mats,
    ) = held
    offset_out, velocity_out, affine_out, deform_out, plastic = results
    (
        move,
        affine8,
        deform8,
        ninth,
        elastic,
        part_a,
        part_b,
        part_c,
        part_d,
        spots_a,
        spots_b,
        weight_hi,
        weight_lo,
        first_w,
        first_d,
        own,
        table,
        leaving,
        speed,
        speed_side,
        speed_out,
        speed_in,
        padded,
        field,
        found_a,
        found_b,
        send_sem,
        recv_sem,
        load_sem,
    ) = work
    loads = [pltpu.make_async_copy(given[k], held[k], load_sem.at[k]) for k in range(12)]
    for copy in loads:
        copy.start()
    me = lax.axis_index("dom")
    barrier = pltpu.get_barrier_semaphore()

    def receives(g):
        return (me + reach(g) >= 0) & (me + reach(g) < length)

    def sends(g):
        return (me - reach(g) >= 0) & (me - reach(g) < length)

    for g in range(GROUPS):

        @pl.when(receives(g))
        def _():
            pl.semaphore_signal(
                barrier,
                inc=1,
                device_id=(partner(me, g, length),),
                device_id_type=pl.DeviceIdType.MESH,
            )

    def start(copy, g):
        @pl.when(receives(g))
        def _():
            copy.start()

    def wait(copy, g):
        @pl.when(sends(g))
        def _():
            copy.wait_recv()

    def wait_sent(copy, g):
        @pl.when(receives(g))
        def _():
            copy.wait_send()

    def partial_copy(step, g):
        return pltpu.make_async_remote_copy(
            src_ref=leaving.at[pl.ds(SENT * g, SENT)],
            dst_ref=table.at[pl.ds(1 + OWN + SLOTS * g, SENT)],
            send_sem=send_sem.at[step, 0, g],
            recv_sem=recv_sem.at[step, 0, g],
            device_id=(partner(me, g, length),),
            device_id_type=pl.DeviceIdType.MESH,
        )

    def speed_copy(step, g):
        return pltpu.make_async_remote_copy(
            src_ref=speed_out.at[pl.ds(3 * g, 3)],
            dst_ref=speed_in.at[pl.ds(3 * g, 3)],
            send_sem=send_sem.at[step, 1, g],
            recv_sem=recv_sem.at[step, 1, g],
            device_id=(partner(me, g, length),),
            device_id_type=pl.DeviceIdType.MESH,
        )

    row_id = lax.broadcasted_iota(jnp.int32, (8, 128), 0)
    lane_id = lax.broadcasted_iota(jnp.int32, (8, 128), 1)
    upper = row_id < 4
    left = lane_id < 64
    diagonal = upper == left
    upper_left = upper & left
    lower_right = diagonal & ~upper
    channel = row_id % 4
    zero_tile = jnp.zeros((8, 128), jnp.float32)

    slot = lane_id + 128 * (row_id % 2)

    def live_slots(r):
        limit = counts[4 * r + 3]
        for k in (2, 1, 0):
            limit = jnp.where(row_id < 2 * k + 2, counts[4 * r + k], limit)
        return slot < limit

    ones = jnp.where((row_id == 0) | (row_id == 4), 1.0, 0.0)

    def load_tile(t, carry):
        lanes = pl.ds(pl.multiple_of(128 * t, 128), 128)
        spot = pl.ds(pl.multiple_of(8 * t, 8), 8)
        move[spot, :] = jnp.concatenate(
            [offset_in[:, lanes], velocity_in[:, lanes], zero_tile[0:2]], axis=0
        )
        affine8[spot, :] = affine_in[0:8, lanes]
        deform8[spot, :] = strain_in[0:8, lanes] + ones
        ninth[spot, :] = jnp.concatenate(
            [affine_in[8:9, lanes], strain_in[8:9, lanes] + 1.0, zero_tile[0:6]], axis=0
        )
        part_b[spot, :] = zero_tile
        part_c[spot, :] = zero_tile
        part_d[spot, :] = zero_tile
        spots_b[spot, :] = zero_tile
        return carry

    for copy in loads:
        copy.wait()
    lax.fori_loop(0, TILES, load_tile, 0, unroll=4)
    plastic[...] = plastic_in[...]
    table[0] = zero_tile
    padded[0] = zero_tile
    for g in range(GROUPS):

        @pl.when(jnp.logical_not(sends(g)))
        def _():
            for k in range(SENT):
                table[1 + OWN + SLOTS * g + k] = zero_tile
            for k in range(3):
                speed_in[3 * g + k] = zero_tile

    def one_step(step, carry):
        def particles(r, carry):
            band = pl.ds(pl.multiple_of(8 * r, 8), 8)

            def every(i):
                return pl.ds(64 * r + i, 8, stride=8)

            f = [deform8[every(k), :] for k in range(8)] + [ninth[every(1), :]]
            volume = determinant(f)
            clamped = jnp.clip(volume, 1.0 - COMPRESS, 1.0 + STRETCH)
            hardened = plastic[band, :] * volume / clamped
            factor = jnp.exp(jnp.log(clamped / volume) / 3.0)
            e = [x * factor for x in f]
            for k in range(9):
                elastic[k, band, :] = e[k]
            elastic[9, band, :] = hardened
            live = live_slots(r)
            mass = jnp.where(live, mass_in[band, :], 0.0)
            stiff = jnp.exp(HARDEN * (1.0 - hardened))
            shear = SHEAR * stiff
            bulk = BULK * stiff * jnp.log(clamped)
            part_a[every(0), :] = mass
            part_a[every(4), :] = mass
            for i in range(3):
                value = mass * move[every(3 + i), :]
                part_a[every(1 + i), :] = value
                part_a[every(5 + i), :] = value
            inner = {}
            for i in range(3):
                for j in range(i, 3):
                    total = (
                        e[3 * i] * e[3 * j]
                        + e[3 * i + 1] * e[3 * j + 1]
                        + e[3 * i + 2] * e[3 * j + 2]
                    )
                    stress = shear * (total - 1.0) + bulk if i == j else shear * total
                    inner[i, j] = inner[j, i] = stress
            for i in range(3):
                for j, target in enumerate((part_b, part_c, part_d)):
                    k = 3 * i + j
                    affine = affine8[every(k), :] if k < 8 else ninth[every(0), :]
                    value = mass * (affine - (4.0 * DT) * inner[i, j])
                    value = jnp.where(live, value, 0.0)
                    target[every(1 + i), :] = value
                    target[every(5 + i), :] = value
            cell = cells[band, :]
            corner = (cell >> 4, (cell >> 2) & 3, cell & 3)
            spots = []
            for i in range(3):
                c = corner[i].astype(jnp.float32)
                frac = 0.5 + move[every(i), :]
                spots += [
                    c,
                    c + frac,
                    0.5 * (1.5 - frac) * (1.5 - frac),
                    0.75 - (frac - 1.0) * (frac - 1.0),
                    0.5 * (frac - 0.5) * (frac - 0.5),
                ]
            for k, value in enumerate(spots):
                if k < 8:
                    spots_a[every(k), :] = value
                else:
                    spots_b[every(k - 8), :] = value
            return carry

        lax.fori_loop(0, TILES // 8, particles, 0)

        def scatter(b, carry):
            mass_flow = pair(part_a, b)
            push = [pair(part_b, b), pair(part_c, b), pair(part_d, b)]
            tile_a = pair(spots_a, b)
            tile_b = pair(spots_b, b)
            lines = [tile_a[k : k + 1] for k in range(8)] + [tile_b[k : k + 1] for k in range(7)]
            first, second, third = lines[0:5], lines[5:10], lines[10:15]
            blocks = [[], [], []]
            weights = []
            for a in range(3):
                node = consts[80 + 8 * a : 88 + 8 * a, :]
                node = jnp.concatenate([node, node], axis=1)
                w = weight(node, first)
                d = w * (node - first[1])
                weights.append((w, d))
                blocks[0].append(w * mass_flow + d * push[0])
                blocks[1].append(w * push[1])
                blocks[2].append(w * push[2])
            spot = pl.ds(pl.multiple_of(24 * b, 8), 24)
            first_w[spot, :] = jnp.concatenate([w for w, d in weights], axis=0)
            first_d[spot, :] = jnp.concatenate([d for w, d in weights], axis=0)
            lhs = jnp.concatenate([jnp.concatenate(x, axis=0) for x in blocks], axis=1)
            node2 = consts[0:40, :]
            node2 = jnp.concatenate([node2, node2], axis=1)
            node3 = consts[40:80, :]
            node3 = jnp.concatenate([node3, node3], axis=1)
            w23 = weight(node2, second) * weight(node3, third)
            rhs = jnp.concatenate(
                [w23, w23 * (node2 - second[1]), w23 * (node3 - third[1])], axis=1
            )
            rhs = jnp.concatenate([rhs, jnp.zeros((8, 3 * PMAX), jnp.float32)], axis=0)
            high = rhs.astype(jnp.bfloat16)
            low = low_part(rhs).astype(jnp.bfloat16)
            spot = pl.ds(pl.multiple_of(48 * b, 16), 48)
            weight_hi[spot, :] = high
            weight_lo[spot, :] = low
            lhs = high_low(lhs, 0)
            both = dot_nt(lhs, high) + dot_nt(lhs, low)
            total = both[0:24] + both[24:48]
            block = jnp.concatenate(
                [
                    total[0:8, 0:36],
                    total[8:16, 0:RIM],
                    total[16:24, 0:RIM],
                    total[8:16, RIM:36],
                    total[16:24, RIM:36],
                    zero_tile[:, 0:20],
                ],
                axis=1,
            )
            own[b] = block
            table[1 + b] = block
            return carry

        lax.fori_loop(0, OWN, scatter, 0, unroll=16)

        @pl.when(step == 0)
        def _():
            pl.semaphore_wait(
                barrier, jnp.minimum(me, HOPS) + jnp.minimum(length - 1 - me, HOPS)
            )

        for g in FAR_FIRST:
            tiles = [own[rows[0, SLOTS * g + k]] for k in range(SLOTS)]
            for m in range(SLOTS - SENT):
                third = tiles[SENT + m]
                for k, by in ((2 * m, USED), (2 * m + 1, 2 * USED - 128)):
                    leaving[SENT * g + k] = jnp.where(
                        lane_id < USED, tiles[k], pltpu.roll(third, by, 1)
                    )
            start(partial_copy(step, g), g)
        for g in NEAR_FIRST:
            wait(partial_copy(step, g), g)
            at = 1 + OWN + SLOTS * g
            for m in range(SLOTS - SENT):
                table[at + SENT + m] = jnp.where(
                    lane_id < 128 - USED,
                    pltpu.roll(table[at + 2 * m], 128 - USED, 1),
                    pltpu.roll(table[at + 2 * m + 1], 256 - 2 * USED, 1),
                )
        for g in FAR_FIRST:
            wait_sent(partial_copy(step, g), g)

        offset_id = consts[104:112, :]

        def collect(o, total):
            here = offset_id == o.astype(jnp.float32)
            return tuple(
                jnp.where(here, table[1 + links[b, o]], total[b]) for b in range(OWN)
            )

        total = lax.fori_loop(0, 27, collect, (zero_tile,) * OWN, unroll=27)
        total = dot_nn(high_low(jnp.concatenate(total, axis=0), 1), fold_mats[0])
        for b in range(OWN):
            node = total[8 * b : 8 * b + 8]
            node = node + pltpu.roll(pltpu.roll(node, 4, 0), 64, 1)
            node = jnp.where(diagonal, node, 0.0)
            mass = jnp.where(channel == 0, node, 0.0)
            mass = mass + pltpu.roll(mass, 1, 0)
            mass = mass + pltpu.roll(mass, 2, 0)
            node = node / jnp.maximum(mass, MASS_FLOOR)
            node = node - jnp.where(channel == 3, DT * GRAVITY, 0.0)
            node = jnp.where(diagonal, node, 0.0)
            speed[b] = node
            speed_side[b] = pltpu.roll(node, 64, 1)

        for g in FAR_FIRST:
            for m in range(3):
                r = [rows[0, SLOTS * g + 4 * m + k] for k in range(4)]
                speed_out[3 * g + m] = jnp.where(upper, speed[r[0]], speed[r[1]]) + jnp.where(
                    upper, speed_side[r[2]], speed_side[r[3]]
                )
            start(speed_copy(step, g), g)

        def spread(tiles):
            x = high_low(jnp.concatenate(tiles, axis=0), 1)
            return dot_nn(x, fold_mats[1]).reshape(len(tiles), 8, 128)

        padded[1 : 1 + OWN] = spread([speed[b] for b in range(OWN)])
        for g in NEAR_FIRST:
            wait(speed_copy(step, g), g)
            tiles = []
            for m in range(3):
                z = speed_in[3 * g + m]
                zs = pltpu.roll(z, 4, 0)
                zl = pltpu.roll(z, 64, 1)
                zd = pltpu.roll(zs, 64, 1)
                tiles.append(jnp.where(upper_left, z, jnp.where(lower_right, zd, 0.0)))
                tiles.append(jnp.where(upper_left, zd, jnp.where(lower_right, z, 0.0)))
                tiles.append(jnp.where(upper_left, zl, jnp.where(lower_right, zs, 0.0)))
                tiles.append(jnp.where(upper_left, zs, jnp.where(lower_right, zl, 0.0)))
            padded[1 + OWN + SLOTS * g : 1 + OWN + SLOTS * (g + 1)] = spread(tiles)

        def fetch(o, total):
            here = offset_id == (26 - o).astype(jnp.float32)
            return tuple(
                jnp.where(here, padded[1 + links[b, o]], total[b]) for b in range(OWN)
            )

        for g in FAR_FIRST:
            wait_sent(speed_copy(step, g), g)

        total = lax.fori_loop(0, 27, fetch, (zero_tile,) * OWN, unroll=27)
        for b in range(OWN):
            field[b] = total[b]

        upper_wide = lax.broadcasted_iota(jnp.int32, (8, PMAX), 0) < 4

        def gather(b, carry):
            v = field[b]
            fill = zero_tile[:, 0:12]
            v = jnp.concatenate(
                [
                    jnp.concatenate([v[:, 0:36], fill], axis=1),
                    jnp.concatenate([v[:, 36:56], v[:, 76:92], fill], axis=1),
                    jnp.concatenate([v[:, 56:76], v[:, 92:108], fill], axis=1),
                ],
                axis=0,
            )
            v = high_low(v, 0)
            spot = pl.ds(pl.multiple_of(48 * b, 16), 48)
            both = dot_nn(v, weight_hi[spot, :]) + dot_nn(v, weight_lo[spot, :])
            result = both[0:24] + both[24:48]
            spot = pl.ds(pl.multiple_of(24 * b, 8), 24)

            def fold(x):
                x = x[0:8] + x[8:16] + x[16:24]
                return x + pltpu.roll(x, 4, 0)

            w = first_w[spot, :]
            plain = fold(w * result[:, 0:PMAX])
            by1 = fold(first_d[spot, :] * result[:, 0:PMAX])
            by2 = fold(w * result[:, PMAX : 2 * PMAX])
            by3 = fold(w * result[:, 2 * PMAX : 3 * PMAX])
            spot = pl.ds(pl.multiple_of(16 * b, 16), 16)
            out = jnp.where(upper_wide, plain, by1)
            found_a[spot, :] = jnp.concatenate([out[:, 0:128], out[:, 128:256]], axis=0)
            out = jnp.where(upper_wide, by2, by3)
            found_b[spot, :] = jnp.concatenate([out[:, 0:128], out[:, 128:256]], axis=0)
            return carry

        lax.fori_loop(0, OWN, gather, 0, unroll=16)

        def finish(r, carry):
            band = pl.ds(pl.multiple_of(8 * r, 8), 8)

            def every(i):
                return pl.ds(64 * r + i, 8, stride=8)

            live = live_slots(r)

            def put(ref, i, value):
                ref[every(i), :] = jnp.where(live, value, ref[every(i), :])

            v = [found_a[every(1 + i), :] for i in range(3)]
            moment = [
                [found_a[every(5 + i), :] for i in range(3)],
                [found_b[every(1 + i), :] for i in range(3)],
                [found_b[every(5 + i), :] for i in range(3)],
            ]
            affine = [4.0 * moment[j][i] for i in range(3) for j in range(3)]
            e = [elastic[k, band, :] for k in range(9)]
            for i in range(3):
                put(move, i, move[every(i), :] + DT * v[i])
                put(move, 3 + i, v[i])
            for i in range(3):
                for j in range(3):
                    k = 3 * i + j
                    total = e[k]
                    for m in range(3):
                        total = total + DT * affine[3 * i + m] * e[3 * m + j]
                    if k < 8:
                        put(affine8, k, affine[k])
                        put(deform8, k, total)
                    else:
                        put(ninth, 0, affine[k])
                        put(ninth, 1, total)
            plastic[band, :] = jnp.where(live, elastic[9, band, :], plastic[band, :])
            return carry

        lax.fori_loop(0, TILES // 8, finish, 0)
        return carry

    lax.fori_loop(0, 2, one_step, 0)

    def store_tile(t, carry):
        lanes = pl.ds(pl.multiple_of(128 * t, 128), 128)
        spot = pl.ds(pl.multiple_of(8 * t, 8), 8)
        value = move[spot, :]
        offset_out[:, lanes] = value[0:3]
        velocity_out[:, lanes] = value[3:6]
        affine_out[0:8, lanes] = affine8[spot, :]
        deform_out[0:8, lanes] = deform8[spot, :]
        value = ninth[spot, :]
        affine_out[8:9, lanes] = value[0:1]
        deform_out[8:9, lanes] = value[1:2]
        return carry

    lax.fori_loop(0, TILES, store_tile, 0, unroll=4)


def hand_over(*refs):
    first, last, held = refs[0:5], refs[5:10], refs[10:15]
    copies = []
    for k in range(5):
        come = pltpu.make_async_copy(first[k], held[k], refs[15].at[0, k])
        leave = pltpu.make_async_copy(held[k], last[k], refs[15].at[1, k])
        copies.append((come, leave))
        come.start()
    for come, leave in copies:
        come.wait()
        leave.start()
    for come, leave in copies:
        leave.wait()


def on_device(
    length,
    base_cell,
    offset,
    velocity,
    affine,
    strain,
    plastic,
    particle_mass,
    counts,
    neighbours,
    send_rows,
):
    consts, folds = tables()
    hbm = pl.BlockSpec(memory_space=pltpu.HBM)
    vmem = pl.BlockSpec(memory_space=pltpu.VMEM)
    f32 = jnp.float32
    i32 = jnp.int32
    tile = pltpu.VMEM((8 * TILES, 128), f32)
    planar = (TILES, 128)
    row3 = (3, PARTICLES)
    row9 = (9, PARTICLES)
    shapes = [jax.ShapeDtypeStruct(x, f32) for x in (row3, row3, row9, row9, planar)]
    outs = pl.pallas_call(
        lambda *refs: step_kernel(length, *refs),
        out_shape=shapes,
        in_specs=[hbm] * 12,
        out_specs=[vmem] * 5,
        scratch_shapes=[
            pltpu.SMEM((OWN, 27), i32),
            pltpu.SMEM((1, RECEIVED), i32),
            pltpu.SMEM((OWN,), i32),
            pltpu.VMEM(planar, i32),
            pltpu.VMEM(row3, f32),
            pltpu.VMEM(row3, f32),
            pltpu.VMEM(row9, f32),
            pltpu.VMEM(row9, f32),
            pltpu.VMEM(planar, f32),
            pltpu.VMEM(planar, f32),
            pltpu.VMEM((112, 128), f32),
            pltpu.VMEM((2, 256, 128), jnp.bfloat16),
            tile,
            tile,
            tile,
            tile,
            pltpu.VMEM((10,) + planar, f32),
            tile,
            tile,
            tile,
            tile,
            tile,
            tile,
            pltpu.VMEM((48 * OWN, 3 * PMAX), jnp.bfloat16),
            pltpu.VMEM((48 * OWN, 3 * PMAX), jnp.bfloat16),
            pltpu.VMEM((24 * OWN, PMAX), f32),
            pltpu.VMEM((24 * OWN, PMAX), f32),
            pltpu.VMEM((OWN, 8, 128), f32),
            pltpu.VMEM((TABLE, 8, 128), f32),
            pltpu.VMEM((SENT * GROUPS, 8, 128), f32),
            pltpu.VMEM((OWN, 8, 128), f32),
            pltpu.VMEM((OWN, 8, 128), f32),
            pltpu.VMEM((3 * GROUPS, 8, 128), f32),
            pltpu.VMEM((3 * GROUPS, 8, 128), f32),
            pltpu.VMEM((TABLE, 8, 128), f32),
            pltpu.VMEM((OWN, 8, 128), f32),
            tile,
            tile,
            pltpu.SemaphoreType.DMA((2, 2, GROUPS)),
            pltpu.SemaphoreType.DMA((2, 2, GROUPS)),
            pltpu.SemaphoreType.DMA((12,)),
        ],
        compiler_params=pltpu.CompilerParams(
            collective_id=0, has_side_effects=True, vmem_limit_bytes=62 * 1024 * 1024
        ),
        name="snow_steps",
    )(
        neighbours,
        send_rows,
        counts,
        base_cell.reshape(planar),
        offset,
        velocity,
        affine,
        strain,
        plastic.reshape(planar),
        particle_mass.reshape(planar),
        jnp.asarray(consts),
        jnp.asarray(folds, dtype=jnp.bfloat16),
    )
    outs = pl.pallas_call(
        hand_over,
        out_shape=shapes,
        in_specs=[hbm] * 5,
        out_specs=[hbm] * 5,
        scratch_shapes=[pltpu.VMEM(x.shape, f32) for x in shapes] + [pltpu.SemaphoreType.DMA((2, 5))],
        compiler_params=pltpu.CompilerParams(vmem_limit_bytes=62 * 1024 * 1024),
        name="hand_over",
    )(*outs)
    return tuple(outs[:4]) + (outs[4].reshape(PARTICLES),)


def solution(mesh):
    length = mesh.shape["dom"]
    wide = P(None, "dom")
    flat = P("dom")
    return jax.shard_map(
        lambda *args: on_device(length, *args),
        mesh=mesh,
        in_specs=(flat, wide, wide, wide, wide, flat, flat, flat, P("dom", None), P("dom", None)),
        out_specs=(wide, wide, wide, wide, flat),
        check_vma=False,
    )
```

```python
import jax
import jax.numpy as jnp
import numpy as np
from jax import lax
from jax.experimental import pallas as pl
from jax.experimental.pallas import tpu as pltpu
from jax.sharding import PartitionSpec as P

OWN = 16
PMAX = 256
HOPS = 4
SLOTS = 12
GROUPS = 2 * HOPS
RECEIVED = GROUPS * SLOTS
TABLE = 1 + OWN + RECEIVED
PARTICLES = OWN * PMAX
TILES = PARTICLES // 128
RIM = 20
USED = 36 + 2 * RIM
SENT = 8
RING = 16
FAR_FIRST = (3, 7, 2, 6, 1, 5, 0, 4)
NEAR_FIRST = (0, 4, 1, 5, 2, 6, 3, 7)

DT = 0.05
SHEAR = 4.0
BULK = 4.0
HARDEN = 10.0
COMPRESS = 0.025
STRETCH = 0.0075
GRAVITY = 1.0
MASS_FLOOR = 0.25


def tables():
    places = [(j2, j3) for j2 in range(6) for j3 in range(6)]
    places.sort(key=lambda x: (x[0] in (1, 2, 3, 4) and x[1] in (1, 2, 3, 4), x))
    lanes = [(0, q) for q in range(36)]
    lanes += [(a, q) for a in (1, 2) for q in range(RIM)]
    lanes += [(a, q) for a in (1, 2) for q in range(RIM, 36)]
    lanes += [(3, 0)] * 20
    half = np.arange(8)[:, None] // 4 + np.zeros((1, 128), int)
    third = np.array([x[0] for x in lanes])[None, :] + 0 * half
    place = np.array([x[1] for x in lanes])[None, :] + 0 * half
    inside = third < 3
    spot2 = np.array([x[0] for x in places])
    spot3 = np.array([x[1] for x in places])
    node = [np.where(half == 0, third, 5 - third), spot2[place], spot3[place]]
    step = [(x == 0).astype(int) - (x == 5).astype(int) for x in node]
    offset_id = 9 * (step[0] + 1) + 3 * (step[1] + 1) + step[2] + 1
    offset_id = np.where(inside, offset_id, 13)
    core = [(x + 3) % 4 for x in node]
    core_id = np.where(inside, 16 * core[0] + 4 * core[1] + core[2], -1)
    fold = np.zeros((128, 128), np.float32)
    for h in range(2):
        for l in range(108):
            fold[l, 64 * h + core_id[4 * h, l]] = 1.0
    wide = np.zeros((40, 128))
    none = [6] * 4
    consts = np.concatenate(
        [
            wide + np.append(spot2, none)[:, None],
            wide + np.append(spot3, none)[:, None],
            np.where(half == 0, 0, 5),
            np.where(half == 0, 1, 4),
            np.where(half == 0, 2, 3),
            offset_id,
        ]
    ).astype(np.int32)
    folds = np.stack([np.concatenate([fold, fold]), np.concatenate([fold.T, fold.T])])
    return consts, folds


def determinant(m):
    return (
        m[0] * (m[4] * m[8] - m[5] * m[7])
        - m[1] * (m[3] * m[8] - m[5] * m[6])
        + m[2] * (m[3] * m[7] - m[4] * m[6])
    )


def low_part(x):
    return x - x.astype(jnp.bfloat16).astype(jnp.float32)


def high_low(x, axis):
    return jnp.concatenate([x, low_part(x)], axis=axis).astype(jnp.bfloat16)


def dot_nt(a, b):
    return lax.dot_general(a, b, (((1,), (1,)), ((), ())), preferred_element_type=jnp.float32)


def dot_nn(a, b):
    return lax.dot_general(a, b, (((1,), (0,)), ((), ())), preferred_element_type=jnp.float32)


def weight(node, spots):
    cell, _, first, second, third = spots
    shift = node - cell
    value = jnp.where(shift == 2.0, third, 0.0)
    value = jnp.where(shift == 1.0, second, value)
    return jnp.where(shift == 0.0, first, value)


def pair(ref, b):
    both = ref[pl.ds(pl.multiple_of(16 * b, 16), 16), :]
    return jnp.concatenate([both[0:8], both[8:16]], axis=1)


def reach(group):
    return group + 1 if group < HOPS else -(group - HOPS + 1)


def partner(me, group, length):
    return lax.rem(me + (reach(group) + length), length)


def step_kernel(length, *refs):
    given, results, held, work = refs[0:12], refs[12:17], refs[17:29], refs[29:]
    (
        links,
        rows,
        counts,
        cells,
        offset_in,
        velocity_in,
        affine_in,
        strain_in,
        plastic_in,
        mass_in,
        consts,
        fold_mats,
    ) = held
    offset_out, velocity_out, affine_out, deform_out, plastic = results
    (
        move,
        affine8,
        deform8,
        ninth,
        elastic,
        part_a,
        part_b,
        part_c,
        part_d,
        spots_a,
        spots_b,
        weight_hi,
        weight_lo,
        first_w,
        first_d,
        own,
        table,
        leaving,
        speed,
        speed_side,
        speed_out,
        speed_in,
        padded,
        field,
        found_a,
        found_b,
        send_sem,
        recv_sem,
        load_sem,
    ) = work
    loads = [pltpu.make_async_copy(given[k], held[k], load_sem.at[k]) for k in range(12)]
    for copy in loads:
        copy.start()
    me = lax.axis_index("dom")
    barrier = pltpu.get_barrier_semaphore()

    def receives(g):
        return (me + reach(g) >= 0) & (me + reach(g) < length)

    def sends(g):
        return (me - reach(g) >= 0) & (me - reach(g) < length)

    for g in range(GROUPS):

        @pl.when(receives(g))
        def _():
            pl.semaphore_signal(
                barrier,
                inc=1,
                device_id=(partner(me, g, length),),
                device_id_type=pl.DeviceIdType.MESH,
            )

    depth = lax.rem(me, RING)

    def in_turn(send):
        @pl.when(depth < RING // 2)
        def _():
            send((7, 6, 5, 4, 3, 2, 1, 0))

        @pl.when(depth >= RING // 2)
        def _():
            send((3, 2, 1, 0, 7, 6, 5, 4))

    def start(copy, g):
        @pl.when(receives(g))
        def _():
            copy.start()

    def wait(copy, g):
        @pl.when(sends(g))
        def _():
            copy.wait_recv()

    def wait_sent(copy, g):
        @pl.when(receives(g))
        def _():
            copy.wait_send()

    def partial_copy(step, g):
        return pltpu.make_async_remote_copy(
            src_ref=leaving.at[pl.ds(SENT * g, SENT)],
            dst_ref=table.at[pl.ds(1 + OWN + SLOTS * g, SENT)],
            send_sem=send_sem.at[step, 0, g],
            recv_sem=recv_sem.at[step, 0, g],
            device_id=(partner(me, g, length),),
            device_id_type=pl.DeviceIdType.MESH,
        )

    def speed_copy(step, g):
        return pltpu.make_async_remote_copy(
            src_ref=speed_out.at[pl.ds(3 * g, 3)],
            dst_ref=speed_in.at[pl.ds(3 * g, 3)],
            send_sem=send_sem.at[step, 1, g],
            recv_sem=recv_sem.at[step, 1, g],
            device_id=(partner(me, g, length),),
            device_id_type=pl.DeviceIdType.MESH,
        )

    row_id = lax.broadcasted_iota(jnp.int32, (8, 128), 0)
    lane_id = lax.broadcasted_iota(jnp.int32, (8, 128), 1)
    upper = row_id < 4
    left = lane_id < 64
    diagonal = upper == left
    upper_left = upper & left
    lower_right = diagonal & ~upper
    channel = row_id % 4
    zero_tile = jnp.zeros((8, 128), jnp.float32)

    slot = lane_id + 128 * (row_id % 2)

    def live_slots(r):
        limit = counts[4 * r + 3]
        for k in (2, 1, 0):
            limit = jnp.where(row_id < 2 * k + 2, counts[4 * r + k], limit)
        return slot < limit

    ones = jnp.where((row_id == 0) | (row_id == 4), 1.0, 0.0)

    def load_tile(t, carry):
        lanes = pl.ds(pl.multiple_of(128 * t, 128), 128)
        spot = pl.ds(pl.multiple_of(8 * t, 8), 8)
        move[spot, :] = jnp.concatenate(
            [offset_in[:, lanes], velocity_in[:, lanes], zero_tile[0:2]], axis=0
        )
        affine8[spot, :] = affine_in[0:8, lanes]
        deform8[spot, :] = strain_in[0:8, lanes] + ones
        ninth[spot, :] = jnp.concatenate(
            [affine_in[8:9, lanes], strain_in[8:9, lanes] + 1.0, zero_tile[0:6]], axis=0
        )
        part_b[spot, :] = zero_tile
        part_c[spot, :] = zero_tile
        part_d[spot, :] = zero_tile
        spots_b[spot, :] = zero_tile
        return carry

    for copy in loads:
        copy.wait()
    lax.fori_loop(0, TILES, load_tile, 0, unroll=4)
    plastic[...] = plastic_in[...]
    table[0] = zero_tile
    padded[0] = zero_tile
    for g in range(GROUPS):

        @pl.when(jnp.logical_not(sends(g)))
        def _():
            for k in range(SENT):
                table[1 + OWN + SLOTS * g + k] = zero_tile
            for k in range(3):
                speed_in[3 * g + k] = zero_tile

    def one_step(step, carry):
        def particles(r, carry):
            band = pl.ds(pl.multiple_of(8 * r, 8), 8)

            def every(i):
                return pl.ds(64 * r + i, 8, stride=8)

            f = [deform8[every(k), :] for k in range(8)] + [ninth[every(1), :]]
            volume = determinant(f)
            clamped = jnp.clip(volume, 1.0 - COMPRESS, 1.0 + STRETCH)
            hardened = plastic[band, :] * volume / clamped
            factor = jnp.exp(jnp.log(clamped / volume) / 3.0)
            e = [x * factor for x in f]
            for k in range(9):
                elastic[k, band, :] = e[k]
            elastic[9, band, :] = hardened
            live = live_slots(r)
            mass = jnp.where(live, mass_in[band, :], 0.0)
            stiff = jnp.exp(HARDEN * (1.0 - hardened))
            shear = SHEAR * stiff
            bulk = BULK * stiff * jnp.log(clamped)
            part_a[every(0), :] = mass
            part_a[every(4), :] = mass
            for i in range(3):
                value = mass * move[every(3 + i), :]
                part_a[every(1 + i), :] = value
                part_a[every(5 + i), :] = value
            inner = {}
            for i in range(3):
                for j in range(i, 3):
                    total = (
                        e[3 * i] * e[3 * j]
                        + e[3 * i + 1] * e[3 * j + 1]
                        + e[3 * i + 2] * e[3 * j + 2]
                    )
                    stress = shear * (total - 1.0) + bulk if i == j else shear * total
                    inner[i, j] = inner[j, i] = stress
            for i in range(3):
                for j, target in enumerate((part_b, part_c, part_d)):
                    k = 3 * i + j
                    affine = affine8[every(k), :] if k < 8 else ninth[every(0), :]
                    value = mass * (affine - (4.0 * DT) * inner[i, j])
                    value = jnp.where(live, value, 0.0)
                    target[every(1 + i), :] = value
                    target[every(5 + i), :] = value
            cell = cells[band, :]
            corner = (cell >> 4, (cell >> 2) & 3, cell & 3)
            spots = []
            for i in range(3):
                c = corner[i].astype(jnp.float32)
                frac = 0.5 + move[every(i), :]
                spots += [
                    c,
                    c + frac,
                    0.5 * (1.5 - frac) * (1.5 - frac),
                    0.75 - (frac - 1.0) * (frac - 1.0),
                    0.5 * (frac - 0.5) * (frac - 0.5),
                ]
            for k, value in enumerate(spots):
                if k < 8:
                    spots_a[every(k), :] = value
                else:
                    spots_b[every(k - 8), :] = value
            return carry

        lax.fori_loop(0, TILES // 8, particles, 0)

        places = lax.broadcasted_iota(jnp.int32, (8, PMAX), 0).astype(jnp.float32)

        def spline_rows(spots):
            w = weight(places, spots)
            return w, w * (places - spots[1])

        def spread_rows(x, at, count):
            parts = []
            for k in range(0, count, 8):
                index = consts[at + k : at + k + 8, :]
                parts.append(
                    jnp.concatenate(
                        [jnp.take_along_axis(x[:, l : l + 128], index, axis=0) for l in (0, 128)],
                        axis=1,
                    )
                )
            return jnp.concatenate(parts, axis=0)

        def scatter(b, carry):
            mass_flow = pair(part_a, b)
            push = [pair(part_b, b), pair(part_c, b), pair(part_d, b)]
            tile_a = pair(spots_a, b)
            tile_b = pair(spots_b, b)
            lines = [tile_a[k : k + 1] for k in range(8)] + [tile_b[k : k + 1] for k in range(7)]
            first, second, third = lines[0:5], lines[5:10], lines[10:15]
            blocks = [[], [], []]
            weights = []
            first_pair = spline_rows(first)
            for a in range(3):
                w, d = (spread_rows(x, 80 + 8 * a, 8) for x in first_pair)
                weights.append((w, d))
                blocks[0].append(w * mass_flow + d * push[0])
                blocks[1].append(w * push[1])
                blocks[2].append(w * push[2])
            spot = pl.ds(pl.multiple_of(24 * b, 8), 24)
            first_w[spot, :] = jnp.concatenate([w for w, d in weights], axis=0)
            first_d[spot, :] = jnp.concatenate([d for w, d in weights], axis=0)
            lhs = jnp.concatenate([jnp.concatenate(x, axis=0) for x in blocks], axis=1)
            second_w, second_d = (spread_rows(x, 0, 40) for x in spline_rows(second))
            third_w, third_d = (spread_rows(x, 40, 40) for x in spline_rows(third))
            rhs = jnp.concatenate(
                [second_w * third_w, second_d * third_w, second_w * third_d], axis=1
            )
            rhs = jnp.concatenate([rhs, jnp.zeros((8, 3 * PMAX), jnp.float32)], axis=0)
            high = rhs.astype(jnp.bfloat16)
            low = low_part(rhs).astype(jnp.bfloat16)
            spot = pl.ds(pl.multiple_of(48 * b, 16), 48)
            weight_hi[spot, :] = high
            weight_lo[spot, :] = low
            lhs = high_low(lhs, 0)
            both = dot_nt(lhs, high) + dot_nt(lhs, low)
            total = both[0:24] + both[24:48]
            block = jnp.concatenate(
                [
                    total[0:8, 0:36],
                    total[8:16, 0:RIM],
                    total[16:24, 0:RIM],
                    total[8:16, RIM:36],
                    total[16:24, RIM:36],
                    zero_tile[:, 0:20],
                ],
                axis=1,
            )
            own[b] = block
            table[1 + b] = block
            return carry

        lax.fori_loop(0, OWN, scatter, 0, unroll=16)

        @pl.when(step == 0)
        def _():
            pl.semaphore_wait(
                barrier, jnp.minimum(me, HOPS) + jnp.minimum(length - 1 - me, HOPS)
            )

        def send_partials(order):
            for g in order:
                tiles = [own[rows[0, SLOTS * g + k]] for k in range(SLOTS)]
                for m in range(SLOTS - SENT):
                    third = tiles[SENT + m]
                    for k, by in ((2 * m, USED), (2 * m + 1, 2 * USED - 128)):
                        leaving[SENT * g + k] = jnp.where(
                            lane_id < USED, tiles[k], pltpu.roll(third, by, 1)
                        )
                start(partial_copy(step, g), g)

        in_turn(send_partials)
        for g in NEAR_FIRST:
            wait(partial_copy(step, g), g)
            at = 1 + OWN + SLOTS * g
            for m in range(SLOTS - SENT):
                table[at + SENT + m] = jnp.where(
                    lane_id < 128 - USED,
                    pltpu.roll(table[at + 2 * m], 128 - USED, 1),
                    pltpu.roll(table[at + 2 * m + 1], 256 - 2 * USED, 1),
                )
        for g in FAR_FIRST:
            wait_sent(partial_copy(step, g), g)

        offset_id = consts[104:112, :]

        def collect(o, total):
            here = offset_id == o
            return tuple(
                jnp.where(here, table[1 + links[b, o]], total[b]) for b in range(OWN)
            )

        total = lax.fori_loop(0, 27, collect, (zero_tile,) * OWN, unroll=27)
        total = dot_nn(high_low(jnp.concatenate(total, axis=0), 1), fold_mats[0])
        for b in range(OWN):
            node = total[8 * b : 8 * b + 8]
            node = node + pltpu.roll(pltpu.roll(node, 4, 0), 64, 1)
            node = jnp.where(diagonal, node, 0.0)
            mass = jnp.where(channel == 0, node, 0.0)
            mass = mass + pltpu.roll(mass, 1, 0)
            mass = mass + pltpu.roll(mass, 2, 0)
            node = node / jnp.maximum(mass, MASS_FLOOR)
            node = node - jnp.where(channel == 3, DT * GRAVITY, 0.0)
            node = jnp.where(diagonal, node, 0.0)
            speed[b] = node
            speed_side[b] = pltpu.roll(node, 64, 1)

        def send_speeds(order):
            for g in order:
                for m in range(3):
                    r = [rows[0, SLOTS * g + 4 * m + k] for k in range(4)]
                    speed_out[3 * g + m] = jnp.where(
                        upper, speed[r[0]], speed[r[1]]
                    ) + jnp.where(upper, speed_side[r[2]], speed_side[r[3]])
                start(speed_copy(step, g), g)

        in_turn(send_speeds)

        def spread(tiles):
            x = high_low(jnp.concatenate(tiles, axis=0), 1)
            return dot_nn(x, fold_mats[1]).reshape(len(tiles), 8, 128)

        padded[1 : 1 + OWN] = spread([speed[b] for b in range(OWN)])
        for batch in (NEAR_FIRST[0:4], NEAR_FIRST[4:8]):
            for g in batch:
                wait(speed_copy(step, g), g)
            tiles = []
            for g in batch:
                for m in range(3):
                    z = speed_in[3 * g + m]
                    zs = pltpu.roll(z, 4, 0)
                    zl = pltpu.roll(z, 64, 1)
                    zd = pltpu.roll(zs, 64, 1)
                    tiles.append(jnp.where(upper_left, z, jnp.where(lower_right, zd, 0.0)))
                    tiles.append(jnp.where(upper_left, zd, jnp.where(lower_right, z, 0.0)))
                    tiles.append(jnp.where(upper_left, zl, jnp.where(lower_right, zs, 0.0)))
                    tiles.append(jnp.where(upper_left, zs, jnp.where(lower_right, zl, 0.0)))
            tiles = spread(tiles)
            for k, g in enumerate(batch):
                at = 1 + OWN + SLOTS * g
                padded[at : at + SLOTS] = tiles[SLOTS * k : SLOTS * (k + 1)]

        def fetch(o, total):
            here = offset_id == 26 - o
            return tuple(
                jnp.where(here, padded[1 + links[b, o]], total[b]) for b in range(OWN)
            )

        for g in FAR_FIRST:
            wait_sent(speed_copy(step, g), g)

        total = lax.fori_loop(0, 27, fetch, (zero_tile,) * OWN, unroll=27)
        for b in range(OWN):
            field[b] = total[b]

        upper_wide = lax.broadcasted_iota(jnp.int32, (8, PMAX), 0) < 4

        def gather(b, carry):
            v = field[b]
            fill = zero_tile[:, 0:12]
            v = jnp.concatenate(
                [
                    jnp.concatenate([v[:, 0:36], fill], axis=1),
                    jnp.concatenate([v[:, 36:56], v[:, 76:92], fill], axis=1),
                    jnp.concatenate([v[:, 56:76], v[:, 92:108], fill], axis=1),
                ],
                axis=0,
            )
            v = high_low(v, 0)
            spot = pl.ds(pl.multiple_of(48 * b, 16), 48)
            both = dot_nn(v, weight_hi[spot, :]) + dot_nn(v, weight_lo[spot, :])
            result = both[0:24] + both[24:48]
            spot = pl.ds(pl.multiple_of(24 * b, 8), 24)

            def fold(x):
                x = x[0:8] + x[8:16] + x[16:24]
                return x + pltpu.roll(x, 4, 0)

            w = first_w[spot, :]
            plain = fold(w * result[:, 0:PMAX])
            by1 = fold(first_d[spot, :] * result[:, 0:PMAX])
            by2 = fold(w * result[:, PMAX : 2 * PMAX])
            by3 = fold(w * result[:, 2 * PMAX : 3 * PMAX])
            spot = pl.ds(pl.multiple_of(16 * b, 16), 16)
            out = jnp.where(upper_wide, plain, by1)
            found_a[spot, :] = jnp.concatenate([out[:, 0:128], out[:, 128:256]], axis=0)
            out = jnp.where(upper_wide, by2, by3)
            found_b[spot, :] = jnp.concatenate([out[:, 0:128], out[:, 128:256]], axis=0)
            return carry

        lax.fori_loop(0, OWN, gather, 0, unroll=16)

        def finish(r, carry):
            band = pl.ds(pl.multiple_of(8 * r, 8), 8)

            def every(i):
                return pl.ds(64 * r + i, 8, stride=8)

            live = live_slots(r)

            def put(ref, i, value):
                ref[every(i), :] = jnp.where(live, value, ref[every(i), :])

            v = [found_a[every(1 + i), :] for i in range(3)]
            moment = [
                [found_a[every(5 + i), :] for i in range(3)],
                [found_b[every(1 + i), :] for i in range(3)],
                [found_b[every(5 + i), :] for i in range(3)],
            ]
            affine = [4.0 * moment[j][i] for i in range(3) for j in range(3)]
            e = [elastic[k, band, :] for k in range(9)]
            for i in range(3):
                put(move, i, move[every(i), :] + DT * v[i])
                put(move, 3 + i, v[i])
            for i in range(3):
                for j in range(3):
                    k = 3 * i + j
                    total = e[k]
                    for m in range(3):
                        total = total + DT * affine[3 * i + m] * e[3 * m + j]
                    if k < 8:
                        put(affine8, k, affine[k])
                        put(deform8, k, total)
                    else:
                        put(ninth, 0, affine[k])
                        put(ninth, 1, total)
            plastic[band, :] = jnp.where(live, elastic[9, band, :], plastic[band, :])
            return carry

        lax.fori_loop(0, TILES // 8, finish, 0)
        return carry

    lax.fori_loop(0, 2, one_step, 0)

    def store_tile(t, carry):
        lanes = pl.ds(pl.multiple_of(128 * t, 128), 128)
        spot = pl.ds(pl.multiple_of(8 * t, 8), 8)
        value = move[spot, :]
        offset_out[:, lanes] = value[0:3]
        velocity_out[:, lanes] = value[3:6]
        affine_out[0:8, lanes] = affine8[spot, :]
        deform_out[0:8, lanes] = deform8[spot, :]
        value = ninth[spot, :]
        affine_out[8:9, lanes] = value[0:1]
        deform_out[8:9, lanes] = value[1:2]
        return carry

    lax.fori_loop(0, TILES, store_tile, 0, unroll=4)


def hand_over(*refs):
    first, last, held = refs[0:5], refs[5:10], refs[10:15]
    copies = []
    for k in range(5):
        come = pltpu.make_async_copy(first[k], held[k], refs[15].at[0, k])
        leave = pltpu.make_async_copy(held[k], last[k], refs[15].at[1, k])
        copies.append((come, leave))
        come.start()
    for come, leave in copies:
        come.wait()
        leave.start()
    for come, leave in copies:
        leave.wait()


def on_device(
    length,
    base_cell,
    offset,
    velocity,
    affine,
    strain,
    plastic,
    particle_mass,
    counts,
    neighbours,
    send_rows,
):
    consts, folds = tables()
    hbm = pl.BlockSpec(memory_space=pltpu.HBM)
    vmem = pl.BlockSpec(memory_space=pltpu.VMEM)
    f32 = jnp.float32
    i32 = jnp.int32
    tile = pltpu.VMEM((8 * TILES, 128), f32)
    planar = (TILES, 128)
    row3 = (3, PARTICLES)
    row9 = (9, PARTICLES)
    shapes = [jax.ShapeDtypeStruct(x, f32) for x in (row3, row3, row9, row9, planar)]
    outs = pl.pallas_call(
        lambda *refs: step_kernel(length, *refs),
        out_shape=shapes,
        in_specs=[hbm] * 12,
        out_specs=[vmem] * 5,
        scratch_shapes=[
            pltpu.SMEM((OWN, 27), i32),
            pltpu.SMEM((1, RECEIVED), i32),
            pltpu.SMEM((OWN,), i32),
            pltpu.VMEM(planar, i32),
            pltpu.VMEM(row3, f32),
            pltpu.VMEM(row3, f32),
            pltpu.VMEM(row9, f32),
            pltpu.VMEM(row9, f32),
            pltpu.VMEM(planar, f32),
            pltpu.VMEM(planar, f32),
            pltpu.VMEM((112, 128), i32),
            pltpu.VMEM((2, 256, 128), jnp.bfloat16),
            tile,
            tile,
            tile,
            tile,
            pltpu.VMEM((10,) + planar, f32),
            tile,
            tile,
            tile,
            tile,
            tile,
            tile,
            pltpu.VMEM((48 * OWN, 3 * PMAX), jnp.bfloat16),
            pltpu.VMEM((48 * OWN, 3 * PMAX), jnp.bfloat16),
            pltpu.VMEM((24 * OWN, PMAX), f32),
            pltpu.VMEM((24 * OWN, PMAX), f32),
            pltpu.VMEM((OWN, 8, 128), f32),
            pltpu.VMEM((TABLE, 8, 128), f32),
            pltpu.VMEM((SENT * GROUPS, 8, 128), f32),
            pltpu.VMEM((OWN, 8, 128), f32),
            pltpu.VMEM((OWN, 8, 128), f32),
            pltpu.VMEM((3 * GROUPS, 8, 128), f32),
            pltpu.VMEM((3 * GROUPS, 8, 128), f32),
            pltpu.VMEM((TABLE, 8, 128), f32),
            pltpu.VMEM((OWN, 8, 128), f32),
            tile,
            tile,
            pltpu.SemaphoreType.DMA((2, 2, GROUPS)),
            pltpu.SemaphoreType.DMA((2, 2, GROUPS)),
            pltpu.SemaphoreType.DMA((12,)),
        ],
        compiler_params=pltpu.CompilerParams(
            collective_id=0, has_side_effects=True, vmem_limit_bytes=62 * 1024 * 1024
        ),
        name="snow_steps",
    )(
        neighbours,
        send_rows,
        counts,
        base_cell.reshape(planar),
        offset,
        velocity,
        affine,
        strain,
        plastic.reshape(planar),
        particle_mass.reshape(planar),
        jnp.asarray(consts),
        jnp.asarray(folds, dtype=jnp.bfloat16),
    )
    outs = pl.pallas_call(
        hand_over,
        out_shape=shapes,
        in_specs=[hbm] * 5,
        out_specs=[hbm] * 5,
        scratch_shapes=[pltpu.VMEM(x.shape, f32) for x in shapes] + [pltpu.SemaphoreType.DMA((2, 5))],
        compiler_params=pltpu.CompilerParams(vmem_limit_bytes=62 * 1024 * 1024),
        name="hand_over",
    )(*outs)
    return tuple(outs[:4]) + (outs[4].reshape(PARTICLES),)


def solution(mesh):
    length = mesh.shape["dom"]
    wide = P(None, "dom")
    flat = P("dom")
    return jax.shard_map(
        lambda *args: on_device(length, *args),
        mesh=mesh,
        in_specs=(flat, wide, wide, wide, wide, flat, flat, flat, P("dom", None), P("dom", None)),
        out_specs=(wide, wide, wide, wide, flat),
        check_vma=False,
    )
```

```python
import jax
import jax.numpy as jnp
import numpy as np
from jax import lax
from jax.experimental import pallas as pl
from jax.experimental.pallas import tpu as pltpu
from jax.sharding import PartitionSpec as P

OWN = 16
PMAX = 256
HOPS = 4
SLOTS = 12
GROUPS = 2 * HOPS
RECEIVED = GROUPS * SLOTS
TABLE = 1 + OWN + RECEIVED
PARTICLES = OWN * PMAX
TILES = PARTICLES // 128
RIM = 20
USED = 36 + 2 * RIM
SENT = 8
RING = 16
FAR_FIRST = (3, 7, 2, 6, 1, 5, 0, 4)
NEAR_FIRST = (0, 4, 1, 5, 2, 6, 3, 7)

DT = 0.05
SHEAR = 4.0
BULK = 4.0
HARDEN = 10.0
COMPRESS = 0.025
STRETCH = 0.0075
GRAVITY = 1.0
MASS_FLOOR = 0.25


def tables():
    places = [(j2, j3) for j2 in range(6) for j3 in range(6)]
    places.sort(key=lambda x: (x[0] in (1, 2, 3, 4) and x[1] in (1, 2, 3, 4), x))
    lanes = [(0, q) for q in range(36)]
    lanes += [(a, q) for a in (1, 2) for q in range(RIM)]
    lanes += [(a, q) for a in (1, 2) for q in range(RIM, 36)]
    lanes += [(3, 0)] * 20
    half = np.arange(8)[:, None] // 4 + np.zeros((1, 128), int)
    third = np.array([x[0] for x in lanes])[None, :] + 0 * half
    place = np.array([x[1] for x in lanes])[None, :] + 0 * half
    inside = third < 3
    spot2 = np.array([x[0] for x in places])
    spot3 = np.array([x[1] for x in places])
    node = [np.where(half == 0, third, 5 - third), spot2[place], spot3[place]]
    step = [(x == 0).astype(int) - (x == 5).astype(int) for x in node]
    offset_id = 9 * (step[0] + 1) + 3 * (step[1] + 1) + step[2] + 1
    offset_id = np.where(inside, offset_id, 13)
    core = [(x + 3) % 4 for x in node]
    core_id = np.where(inside, 16 * core[0] + 4 * core[1] + core[2], -1)
    fold = np.zeros((128, 128), np.float32)
    for h in range(2):
        for l in range(108):
            fold[l, 64 * h + core_id[4 * h, l]] = 1.0
    wide = np.zeros((40, 128))
    none = [6] * 4
    consts = np.concatenate(
        [
            wide + np.append(spot2, none)[:, None],
            wide + np.append(spot3, none)[:, None],
            np.where(half == 0, 0, 5),
            np.where(half == 0, 1, 4),
            np.where(half == 0, 2, 3),
            offset_id,
        ]
    ).astype(np.int32)
    folds = np.stack([np.concatenate([fold, fold]), np.concatenate([fold.T, fold.T])])
    return consts, folds


def determinant(m):
    return (
        m[0] * (m[4] * m[8] - m[5] * m[7])
        - m[1] * (m[3] * m[8] - m[5] * m[6])
        + m[2] * (m[3] * m[7] - m[4] * m[6])
    )


def low_part(x):
    return x - x.astype(jnp.bfloat16).astype(jnp.float32)


def high_low(x, axis):
    return jnp.concatenate([x, low_part(x)], axis=axis).astype(jnp.bfloat16)


def dot_nt(a, b):
    return lax.dot_general(a, b, (((1,), (1,)), ((), ())), preferred_element_type=jnp.float32)


def dot_nn(a, b):
    return lax.dot_general(a, b, (((1,), (0,)), ((), ())), preferred_element_type=jnp.float32)


def weight(node, spots):
    cell, _, first, second, third = spots
    shift = node - cell
    value = jnp.where(shift == 2.0, third, 0.0)
    value = jnp.where(shift == 1.0, second, value)
    return jnp.where(shift == 0.0, first, value)


def pair(ref, b):
    both = ref[pl.ds(pl.multiple_of(16 * b, 16), 16), :]
    return jnp.concatenate([both[0:8], both[8:16]], axis=1)


def reach(group):
    return group + 1 if group < HOPS else -(group - HOPS + 1)


def partner(me, group, length):
    return lax.rem(me + (reach(group) + length), length)


def step_kernel(length, *refs):
    given, results, held, work = refs[0:12], refs[12:17], refs[17:29], refs[29:]
    (
        links,
        rows,
        counts,
        cells,
        offset_in,
        velocity_in,
        affine_in,
        strain_in,
        plastic_in,
        mass_in,
        consts,
        fold_mats,
    ) = held
    offset_out, velocity_out, affine_out, deform_out, plastic = results
    (
        move,
        affine8,
        deform8,
        ninth,
        elastic,
        part_a,
        part_b,
        part_c,
        part_d,
        spots_a,
        spots_b,
        products,
        first_w,
        first_d,
        own,
        table,
        leaving,
        speed,
        speed_side,
        speed_out,
        speed_in,
        padded,
        field,
        found_a,
        found_b,
        send_sem,
        recv_sem,
        load_sem,
    ) = work
    me = lax.axis_index("dom")
    barrier = pltpu.get_barrier_semaphore()

    def receives(g):
        return (me + reach(g) >= 0) & (me + reach(g) < length)

    def sends(g):
        return (me - reach(g) >= 0) & (me - reach(g) < length)

    for g in range(GROUPS):

        @pl.when(receives(g))
        def _():
            pl.semaphore_signal(
                barrier,
                inc=1,
                device_id=(partner(me, g, length),),
                device_id_type=pl.DeviceIdType.MESH,
            )

    loads = [pltpu.make_async_copy(given[k], held[k], load_sem.at[k]) for k in range(12)]
    for copy in loads:
        copy.start()

    depth = lax.rem(me, RING)

    def in_turn(send):
        @pl.when(depth < RING // 2)
        def _():
            send((7, 6, 5, 4, 3, 2, 1, 0))

        @pl.when(depth >= RING // 2)
        def _():
            send((3, 2, 1, 0, 7, 6, 5, 4))

    def start(copy, g):
        @pl.when(receives(g))
        def _():
            copy.start()

    def wait(copy, g):
        @pl.when(sends(g))
        def _():
            copy.wait_recv()

    def wait_sent(copy, g):
        @pl.when(receives(g))
        def _():
            copy.wait_send()

    def partial_copy(step, g):
        return pltpu.make_async_remote_copy(
            src_ref=leaving.at[pl.ds(SENT * g, SENT)],
            dst_ref=table.at[pl.ds(1 + OWN + SLOTS * g, SENT)],
            send_sem=send_sem.at[step, 0, g],
            recv_sem=recv_sem.at[step, 0, g],
            device_id=(partner(me, g, length),),
            device_id_type=pl.DeviceIdType.MESH,
        )

    def speed_copy(step, g):
        return pltpu.make_async_remote_copy(
            src_ref=speed_out.at[pl.ds(3 * g, 3)],
            dst_ref=speed_in.at[pl.ds(3 * g, 3)],
            send_sem=send_sem.at[step, 1, g],
            recv_sem=recv_sem.at[step, 1, g],
            device_id=(partner(me, g, length),),
            device_id_type=pl.DeviceIdType.MESH,
        )

    row_id = lax.broadcasted_iota(jnp.int32, (8, 128), 0)
    lane_id = lax.broadcasted_iota(jnp.int32, (8, 128), 1)
    upper = row_id < 4
    left = lane_id < 64
    diagonal = upper == left
    upper_left = upper & left
    lower_right = diagonal & ~upper
    channel = row_id % 4
    zero_tile = jnp.zeros((8, 128), jnp.float32)

    slot = lane_id + 128 * (row_id % 2)

    def live_slots(r):
        limit = counts[4 * r + 3]
        for k in (2, 1, 0):
            limit = jnp.where(row_id < 2 * k + 2, counts[4 * r + k], limit)
        return slot < limit

    ones = jnp.where((row_id == 0) | (row_id == 4), 1.0, 0.0)

    def load_tile(t, carry):
        lanes = pl.ds(pl.multiple_of(128 * t, 128), 128)
        spot = pl.ds(pl.multiple_of(8 * t, 8), 8)
        move[spot, :] = jnp.concatenate(
            [offset_in[:, lanes], velocity_in[:, lanes], zero_tile[0:2]], axis=0
        )
        affine8[spot, :] = affine_in[0:8, lanes]
        deform8[spot, :] = strain_in[0:8, lanes] + ones
        ninth[spot, :] = jnp.concatenate(
            [affine_in[8:9, lanes], strain_in[8:9, lanes] + 1.0, zero_tile[0:6]], axis=0
        )
        part_b[spot, :] = zero_tile
        part_c[spot, :] = zero_tile
        part_d[spot, :] = zero_tile
        spots_b[spot, :] = zero_tile
        return carry

    for copy in loads:
        copy.wait()
    lax.fori_loop(0, TILES, load_tile, 0, unroll=4)
    plastic[...] = plastic_in[...]
    table[0] = zero_tile
    padded[0] = zero_tile
    for g in range(GROUPS):

        @pl.when(jnp.logical_not(sends(g)))
        def _():
            for k in range(SENT):
                table[1 + OWN + SLOTS * g + k] = zero_tile
            for k in range(3):
                speed_in[3 * g + k] = zero_tile

    def one_step(step, carry):
        def particles(r, carry):
            band = pl.ds(pl.multiple_of(8 * r, 8), 8)

            def every(i):
                return pl.ds(64 * r + i, 8, stride=8)

            f = [deform8[every(k), :] for k in range(8)] + [ninth[every(1), :]]
            volume = determinant(f)
            clamped = jnp.clip(volume, 1.0 - COMPRESS, 1.0 + STRETCH)
            hardened = plastic[band, :] * volume / clamped
            factor = jnp.exp(jnp.log(clamped / volume) / 3.0)
            e = [x * factor for x in f]
            for k in range(9):
                elastic[k, band, :] = e[k]
            elastic[9, band, :] = hardened
            live = live_slots(r)
            mass = jnp.where(live, mass_in[band, :], 0.0)
            stiff = jnp.exp(HARDEN * (1.0 - hardened))
            shear = SHEAR * stiff
            bulk = BULK * stiff * jnp.log(clamped)
            part_a[every(0), :] = mass
            part_a[every(4), :] = mass
            for i in range(3):
                value = mass * move[every(3 + i), :]
                part_a[every(1 + i), :] = value
                part_a[every(5 + i), :] = value
            inner = {}
            for i in range(3):
                for j in range(i, 3):
                    total = (
                        e[3 * i] * e[3 * j]
                        + e[3 * i + 1] * e[3 * j + 1]
                        + e[3 * i + 2] * e[3 * j + 2]
                    )
                    stress = shear * (total - 1.0) + bulk if i == j else shear * total
                    inner[i, j] = inner[j, i] = stress
            for i in range(3):
                for j, target in enumerate((part_b, part_c, part_d)):
                    k = 3 * i + j
                    affine = affine8[every(k), :] if k < 8 else ninth[every(0), :]
                    value = mass * (affine - (4.0 * DT) * inner[i, j])
                    value = jnp.where(live, value, 0.0)
                    target[every(1 + i), :] = value
                    target[every(5 + i), :] = value
            cell = cells[band, :]
            corner = (cell >> 4, (cell >> 2) & 3, cell & 3)
            spots = []
            for i in range(3):
                c = corner[i].astype(jnp.float32)
                frac = 0.5 + move[every(i), :]
                spots += [
                    c,
                    c + frac,
                    0.5 * (1.5 - frac) * (1.5 - frac),
                    0.75 - (frac - 1.0) * (frac - 1.0),
                    0.5 * (frac - 0.5) * (frac - 0.5),
                ]
            for k, value in enumerate(spots):
                if k < 8:
                    spots_a[every(k), :] = value
                else:
                    spots_b[every(k - 8), :] = value
            return carry

        lax.fori_loop(0, TILES // 8, particles, 0)

        places = lax.broadcasted_iota(jnp.int32, (8, PMAX), 0).astype(jnp.float32)

        def spline_rows(spots):
            w = weight(places, spots)
            return w, w * (places - spots[1])

        def spread_rows(x, at, count):
            parts = []
            for k in range(0, count, 8):
                index = consts[at + k : at + k + 8, :]
                parts.append(
                    jnp.concatenate(
                        [jnp.take_along_axis(x[:, l : l + 128], index, axis=0) for l in (0, 128)],
                        axis=1,
                    )
                )
            return jnp.concatenate(parts, axis=0)

        def scatter(b, carry):
            mass_flow = pair(part_a, b)
            push = [pair(part_b, b), pair(part_c, b), pair(part_d, b)]
            tile_a = pair(spots_a, b)
            tile_b = pair(spots_b, b)
            lines = [tile_a[k : k + 1] for k in range(8)] + [tile_b[k : k + 1] for k in range(7)]
            first, second, third = lines[0:5], lines[5:10], lines[10:15]
            blocks = [[], [], []]
            weights = []
            first_pair = spline_rows(first)
            for a in range(3):
                w, d = (spread_rows(x, 80 + 8 * a, 8) for x in first_pair)
                weights.append((w, d))
                blocks[0].append(w * mass_flow + d * push[0])
                blocks[1].append(w * push[1])
                blocks[2].append(w * push[2])
            spot = pl.ds(pl.multiple_of(24 * b, 8), 24)
            first_w[spot, :] = jnp.concatenate([w for w, d in weights], axis=0)
            first_d[spot, :] = jnp.concatenate([d for w, d in weights], axis=0)
            lhs = jnp.concatenate([jnp.concatenate(x, axis=0) for x in blocks], axis=1)
            second_w, second_d = (spread_rows(x, 0, 40) for x in spline_rows(second))
            third_w, third_d = (spread_rows(x, 40, 40) for x in spline_rows(third))
            rhs = jnp.concatenate(
                [second_w * third_w, second_d * third_w, second_w * third_d], axis=1
            )
            rhs = jnp.concatenate([rhs, jnp.zeros((8, 3 * PMAX), jnp.float32)], axis=0)
            rhs = high_low(rhs, 0)
            products[pl.ds(pl.multiple_of(96 * b, 16), 96), :] = rhs
            lhs = high_low(lhs, 0)
            both = dot_nt(lhs, rhs[0:48]) + dot_nt(lhs, rhs[48:96])
            total = both[0:24] + both[24:48]
            block = jnp.concatenate(
                [
                    total[0:8, 0:36],
                    total[8:16, 0:RIM],
                    total[16:24, 0:RIM],
                    total[8:16, RIM:36],
                    total[16:24, RIM:36],
                    zero_tile[:, 0:20],
                ],
                axis=1,
            )
            own[b] = block
            table[1 + b] = block
            return carry

        lax.fori_loop(0, OWN, scatter, 0, unroll=16)

        @pl.when(step == 0)
        def _():
            pl.semaphore_wait(
                barrier, jnp.minimum(me, HOPS) + jnp.minimum(length - 1 - me, HOPS)
            )

        def send_partials(order):
            for g in order:
                tiles = [own[rows[0, SLOTS * g + k]] for k in range(SLOTS)]
                for m in range(SLOTS - SENT):
                    third = tiles[SENT + m]
                    for k, by in ((2 * m, USED), (2 * m + 1, 2 * USED - 128)):
                        leaving[SENT * g + k] = jnp.where(
                            lane_id < USED, tiles[k], pltpu.roll(third, by, 1)
                        )
                start(partial_copy(step, g), g)

        in_turn(send_partials)

        @pl.when(step == 1)
        def _():
            for g in FAR_FIRST:
                wait_sent(speed_copy(0, g), g)

        for g in NEAR_FIRST:
            wait(partial_copy(step, g), g)
        for g in range(GROUPS):
            at = 1 + OWN + SLOTS * g
            for m in range(SLOTS - SENT):
                table[at + SENT + m] = jnp.where(
                    lane_id < 128 - USED,
                    pltpu.roll(table[at + 2 * m], 128 - USED, 1),
                    pltpu.roll(table[at + 2 * m + 1], 256 - 2 * USED, 1),
                )

        offset_id = consts[104:112, :]

        def collect(o, total):
            here = offset_id == o
            return tuple(
                jnp.where(here, table[1 + links[b, o]], total[b]) for b in range(OWN)
            )

        total = lax.fori_loop(0, 27, collect, (zero_tile,) * OWN, unroll=27)
        total = dot_nn(high_low(jnp.concatenate(total, axis=0), 1), fold_mats[0])
        for b in range(OWN):
            node = total[8 * b : 8 * b + 8]
            node = node + pltpu.roll(pltpu.roll(node, 4, 0), 64, 1)
            node = jnp.where(diagonal, node, 0.0)
            mass = jnp.where(channel == 0, node, 0.0)
            mass = mass + pltpu.roll(mass, 1, 0)
            mass = mass + pltpu.roll(mass, 2, 0)
            node = node / jnp.maximum(mass, MASS_FLOOR)
            node = node - jnp.where(channel == 3, DT * GRAVITY, 0.0)
            node = jnp.where(diagonal, node, 0.0)
            speed[b] = node
            speed_side[b] = pltpu.roll(node, 64, 1)

        def send_speeds(order):
            for g in order:
                for m in range(3):
                    r = [rows[0, SLOTS * g + 4 * m + k] for k in range(4)]
                    speed_out[3 * g + m] = jnp.where(
                        upper, speed[r[0]], speed[r[1]]
                    ) + jnp.where(upper, speed_side[r[2]], speed_side[r[3]])
                start(speed_copy(step, g), g)

        in_turn(send_speeds)
        for g in FAR_FIRST:
            wait_sent(partial_copy(step, g), g)

        def spread(tiles):
            x = high_low(jnp.concatenate(tiles, axis=0), 1)
            return dot_nn(x, fold_mats[1]).reshape(len(tiles), 8, 128)

        padded[1 : 1 + OWN] = spread([speed[b] for b in range(OWN)])
        for batch in (NEAR_FIRST[0:4], NEAR_FIRST[4:8]):
            for g in batch:
                wait(speed_copy(step, g), g)
            tiles = []
            for g in batch:
                for m in range(3):
                    z = speed_in[3 * g + m]
                    zs = pltpu.roll(z, 4, 0)
                    zl = pltpu.roll(z, 64, 1)
                    zd = pltpu.roll(zs, 64, 1)
                    tiles.append(jnp.where(upper_left, z, jnp.where(lower_right, zd, 0.0)))
                    tiles.append(jnp.where(upper_left, zd, jnp.where(lower_right, z, 0.0)))
                    tiles.append(jnp.where(upper_left, zl, jnp.where(lower_right, zs, 0.0)))
                    tiles.append(jnp.where(upper_left, zs, jnp.where(lower_right, zl, 0.0)))
            tiles = spread(tiles)
            for k, g in enumerate(batch):
                at = 1 + OWN + SLOTS * g
                padded[at : at + SLOTS] = tiles[SLOTS * k : SLOTS * (k + 1)]

        def fetch(o, total):
            here = offset_id == 26 - o
            return tuple(
                jnp.where(here, padded[1 + links[b, o]], total[b]) for b in range(OWN)
            )

        total = lax.fori_loop(0, 27, fetch, (zero_tile,) * OWN, unroll=27)
        for b in range(OWN):
            field[b] = total[b]

        upper_wide = lax.broadcasted_iota(jnp.int32, (8, PMAX), 0) < 4

        def gather(b, carry):
            v = field[b]
            fill = zero_tile[:, 0:12]
            v = jnp.concatenate(
                [
                    jnp.concatenate([v[:, 0:36], fill], axis=1),
                    jnp.concatenate([v[:, 36:56], v[:, 76:92], fill], axis=1),
                    jnp.concatenate([v[:, 56:76], v[:, 92:108], fill], axis=1),
                ],
                axis=0,
            )
            v = high_low(jnp.concatenate([v, v], axis=1), 0)
            both = dot_nn(v, products[pl.ds(pl.multiple_of(96 * b, 16), 96), :])
            result = both[0:24] + both[24:48]
            spot = pl.ds(pl.multiple_of(24 * b, 8), 24)

            def fold(x):
                x = x[0:8] + x[8:16] + x[16:24]
                return x + pltpu.roll(x, 4, 0)

            w = first_w[spot, :]
            plain = fold(w * result[:, 0:PMAX])
            by1 = fold(first_d[spot, :] * result[:, 0:PMAX])
            by2 = fold(w * result[:, PMAX : 2 * PMAX])
            by3 = fold(w * result[:, 2 * PMAX : 3 * PMAX])
            spot = pl.ds(pl.multiple_of(16 * b, 16), 16)
            out = jnp.where(upper_wide, plain, by1)
            found_a[spot, :] = jnp.concatenate([out[:, 0:128], out[:, 128:256]], axis=0)
            out = jnp.where(upper_wide, by2, by3)
            found_b[spot, :] = jnp.concatenate([out[:, 0:128], out[:, 128:256]], axis=0)
            return carry

        lax.fori_loop(0, OWN, gather, 0, unroll=16)

        def finish(r, carry):
            band = pl.ds(pl.multiple_of(8 * r, 8), 8)

            def every(i):
                return pl.ds(64 * r + i, 8, stride=8)

            live = live_slots(r)

            def put(ref, i, value):
                ref[every(i), :] = jnp.where(live, value, ref[every(i), :])

            v = [found_a[every(1 + i), :] for i in range(3)]
            moment = [
                [found_a[every(5 + i), :] for i in range(3)],
                [found_b[every(1 + i), :] for i in range(3)],
                [found_b[every(5 + i), :] for i in range(3)],
            ]
            affine = [4.0 * moment[j][i] for i in range(3) for j in range(3)]
            e = [elastic[k, band, :] for k in range(9)]
            for i in range(3):
                put(move, i, move[every(i), :] + DT * v[i])
                put(move, 3 + i, v[i])
            for i in range(3):
                for j in range(3):
                    k = 3 * i + j
                    total = e[k]
                    for m in range(3):
                        total = total + DT * affine[3 * i + m] * e[3 * m + j]
                    if k < 8:
                        put(affine8, k, affine[k])
                        put(deform8, k, total)
                    else:
                        put(ninth, 0, affine[k])
                        put(ninth, 1, total)
            plastic[band, :] = jnp.where(live, elastic[9, band, :], plastic[band, :])
            return carry

        lax.fori_loop(0, TILES // 8, finish, 0)
        return carry

    lax.fori_loop(0, 2, one_step, 0)
    for g in FAR_FIRST:
        wait_sent(speed_copy(1, g), g)

    def store_tile(t, carry):
        lanes = pl.ds(pl.multiple_of(128 * t, 128), 128)
        spot = pl.ds(pl.multiple_of(8 * t, 8), 8)
        value = move[spot, :]
        offset_out[:, lanes] = value[0:3]
        velocity_out[:, lanes] = value[3:6]
        affine_out[0:8, lanes] = affine8[spot, :]
        deform_out[0:8, lanes] = deform8[spot, :]
        value = ninth[spot, :]
        affine_out[8:9, lanes] = value[0:1]
        deform_out[8:9, lanes] = value[1:2]
        return carry

    lax.fori_loop(0, TILES, store_tile, 0, unroll=4)


def hand_over(*refs):
    first, last, held = refs[0:5], refs[5:10], refs[10:15]
    copies = []
    for k in range(5):
        come = pltpu.make_async_copy(first[k], held[k], refs[15].at[0, k])
        leave = pltpu.make_async_copy(held[k], last[k], refs[15].at[1, k])
        copies.append((come, leave))
        come.start()
    for come, leave in copies:
        come.wait()
        leave.start()
    for come, leave in copies:
        leave.wait()


def on_device(
    length,
    base_cell,
    offset,
    velocity,
    affine,
    strain,
    plastic,
    particle_mass,
    counts,
    neighbours,
    send_rows,
):
    consts, folds = tables()
    hbm = pl.BlockSpec(memory_space=pltpu.HBM)
    vmem = pl.BlockSpec(memory_space=pltpu.VMEM)
    f32 = jnp.float32
    i32 = jnp.int32
    tile = pltpu.VMEM((8 * TILES, 128), f32)
    planar = (TILES, 128)
    row3 = (3, PARTICLES)
    row9 = (9, PARTICLES)
    shapes = [jax.ShapeDtypeStruct(x, f32) for x in (row3, row3, row9, row9, planar)]
    outs = pl.pallas_call(
        lambda *refs: step_kernel(length, *refs),
        out_shape=shapes,
        in_specs=[hbm] * 12,
        out_specs=[vmem] * 5,
        scratch_shapes=[
            pltpu.SMEM((OWN, 27), i32),
            pltpu.SMEM((1, RECEIVED), i32),
            pltpu.SMEM((OWN,), i32),
            pltpu.VMEM(planar, i32),
            pltpu.VMEM(row3, f32),
            pltpu.VMEM(row3, f32),
            pltpu.VMEM(row9, f32),
            pltpu.VMEM(row9, f32),
            pltpu.VMEM(planar, f32),
            pltpu.VMEM(planar, f32),
            pltpu.VMEM((112, 128), i32),
            pltpu.VMEM((2, 256, 128), jnp.bfloat16),
            tile,
            tile,
            tile,
            tile,
            pltpu.VMEM((10,) + planar, f32),
            tile,
            tile,
            tile,
            tile,
            tile,
            tile,
            pltpu.VMEM((96 * OWN, 3 * PMAX), jnp.bfloat16),
            pltpu.VMEM((24 * OWN, PMAX), f32),
            pltpu.VMEM((24 * OWN, PMAX), f32),
            pltpu.VMEM((OWN, 8, 128), f32),
            pltpu.VMEM((TABLE, 8, 128), f32),
            pltpu.VMEM((SENT * GROUPS, 8, 128), f32),
            pltpu.VMEM((OWN, 8, 128), f32),
            pltpu.VMEM((OWN, 8, 128), f32),
            pltpu.VMEM((3 * GROUPS, 8, 128), f32),
            pltpu.VMEM((3 * GROUPS, 8, 128), f32),
            pltpu.VMEM((TABLE, 8, 128), f32),
            pltpu.VMEM((OWN, 8, 128), f32),
            tile,
            tile,
            pltpu.SemaphoreType.DMA((2, 2, GROUPS)),
            pltpu.SemaphoreType.DMA((2, 2, GROUPS)),
            pltpu.SemaphoreType.DMA((12,)),
        ],
        compiler_params=pltpu.CompilerParams(
            collective_id=0, has_side_effects=True, vmem_limit_bytes=62 * 1024 * 1024
        ),
        name="snow_steps",
    )(
        neighbours,
        send_rows,
        counts,
        base_cell.reshape(planar),
        offset,
        velocity,
        affine,
        strain,
        plastic.reshape(planar),
        particle_mass.reshape(planar),
        jnp.asarray(consts),
        jnp.asarray(folds, dtype=jnp.bfloat16),
    )
    outs = pl.pallas_call(
        hand_over,
        out_shape=shapes,
        in_specs=[hbm] * 5,
        out_specs=[hbm] * 5,
        scratch_shapes=[pltpu.VMEM(x.shape, f32) for x in shapes] + [pltpu.SemaphoreType.DMA((2, 5))],
        compiler_params=pltpu.CompilerParams(vmem_limit_bytes=62 * 1024 * 1024),
        name="hand_over",
    )(*outs)
    return tuple(outs[:4]) + (outs[4].reshape(PARTICLES),)


def solution(mesh):
    length = mesh.shape["dom"]
    wide = P(None, "dom")
    flat = P("dom")
    return jax.shard_map(
        lambda *args: on_device(length, *args),
        mesh=mesh,
        in_specs=(flat, wide, wide, wide, wide, flat, flat, flat, P("dom", None), P("dom", None)),
        out_specs=(wide, wide, wide, wide, flat),
        check_vma=False,
    )
```

```python
import jax
import jax.numpy as jnp
import numpy as np
from jax import lax
from jax.experimental import pallas as pl
from jax.experimental.pallas import tpu as pltpu
from jax.sharding import PartitionSpec as P

OWN = 16
PMAX = 256
HOPS = 4
SLOTS = 12
GROUPS = 2 * HOPS
RECEIVED = GROUPS * SLOTS
TABLE = 1 + OWN + RECEIVED
PARTICLES = OWN * PMAX
TILES = PARTICLES // 128
RIM = 20
USED = 36 + 2 * RIM
SENT = 8
RING = 16
OTHERS = tuple(o for o in range(27) if o != 13)
FAR_FIRST = (3, 7, 2, 6, 1, 5, 0, 4)
NEAR_FIRST = (0, 4, 1, 5, 2, 6, 3, 7)

DT = 0.05
SHEAR = 4.0
BULK = 4.0
HARDEN = 10.0
COMPRESS = 0.025
STRETCH = 0.0075
GRAVITY = 1.0
MASS_FLOOR = 0.25


def tables():
    places = [(j2, j3) for j2 in range(6) for j3 in range(6)]
    places.sort(key=lambda x: (x[0] in (1, 2, 3, 4) and x[1] in (1, 2, 3, 4), x))
    lanes = [(0, q) for q in range(36)]
    lanes += [(a, q) for a in (1, 2) for q in range(RIM)]
    lanes += [(a, q) for a in (1, 2) for q in range(RIM, 36)]
    lanes += [(3, 0)] * 20
    half = np.arange(8)[:, None] // 4 + np.zeros((1, 128), int)
    third = np.array([x[0] for x in lanes])[None, :] + 0 * half
    place = np.array([x[1] for x in lanes])[None, :] + 0 * half
    inside = third < 3
    spot2 = np.array([x[0] for x in places])
    spot3 = np.array([x[1] for x in places])
    node = [np.where(half == 0, third, 5 - third), spot2[place], spot3[place]]
    step = [(x == 0).astype(int) - (x == 5).astype(int) for x in node]
    offset_id = 9 * (step[0] + 1) + 3 * (step[1] + 1) + step[2] + 1
    offset_id = np.where(inside, offset_id, 13)
    core = [(x + 3) % 4 for x in node]
    core_id = np.where(inside, 16 * core[0] + 4 * core[1] + core[2], -1)
    fold = np.zeros((128, 128), np.float32)
    for h in range(2):
        for l in range(108):
            fold[l, 64 * h + core_id[4 * h, l]] = 1.0
    wide = np.zeros((40, 128))
    none = [6] * 4
    consts = np.concatenate(
        [
            wide + np.append(spot2, none)[:, None],
            wide + np.append(spot3, none)[:, None],
            np.where(half == 0, 0, 5),
            np.where(half == 0, 1, 4),
            np.where(half == 0, 2, 3),
            offset_id,
        ]
    ).astype(np.int32)
    folds = np.stack([np.concatenate([fold, fold]), np.concatenate([fold.T, fold.T])])
    return consts, folds


def determinant(m):
    return (
        m[0] * (m[4] * m[8] - m[5] * m[7])
        - m[1] * (m[3] * m[8] - m[5] * m[6])
        + m[2] * (m[3] * m[7] - m[4] * m[6])
    )


def low_part(x):
    return x - x.astype(jnp.bfloat16).astype(jnp.float32)


def high_low(x, axis):
    return jnp.concatenate([x, low_part(x)], axis=axis).astype(jnp.bfloat16)


def dot_nt(a, b):
    return lax.dot_general(a, b, (((1,), (1,)), ((), ())), preferred_element_type=jnp.float32)


def dot_nn(a, b):
    return lax.dot_general(a, b, (((1,), (0,)), ((), ())), preferred_element_type=jnp.float32)


def weight(node, spots):
    cell, _, first, second, third = spots
    shift = node - cell
    value = jnp.where(shift == 2.0, third, 0.0)
    value = jnp.where(shift == 1.0, second, value)
    return jnp.where(shift == 0.0, first, value)


def pair(ref, b):
    both = ref[pl.ds(pl.multiple_of(16 * b, 16), 16), :]
    return jnp.concatenate([both[0:8], both[8:16]], axis=1)


def reach(group):
    return group + 1 if group < HOPS else -(group - HOPS + 1)


def partner(me, group, length):
    return lax.rem(me + (reach(group) + length), length)


def step_kernel(length, *refs):
    given, results, held, work = refs[0:12], refs[12:17], refs[17:29], refs[29:]
    (
        links,
        rows,
        counts,
        cells,
        offset_in,
        velocity_in,
        affine_in,
        strain_in,
        plastic_in,
        mass_in,
        consts,
        fold_mats,
    ) = held
    offset_out, velocity_out, affine_out, deform_out, plastic = results
    (
        move,
        affine8,
        deform8,
        ninth,
        elastic,
        part_a,
        part_b,
        part_c,
        part_d,
        spots_a,
        spots_b,
        products,
        first_w,
        first_d,
        own,
        table,
        leaving,
        speed,
        speed_side,
        speed_out,
        speed_in,
        padded,
        field,
        found_a,
        found_b,
        send_sem,
        recv_sem,
        load_sem,
    ) = work
    me = lax.axis_index("dom")
    barrier = pltpu.get_barrier_semaphore()

    def receives(g):
        return (me + reach(g) >= 0) & (me + reach(g) < length)

    def sends(g):
        return (me - reach(g) >= 0) & (me - reach(g) < length)

    for g in range(GROUPS):

        @pl.when(receives(g))
        def _():
            pl.semaphore_signal(
                barrier,
                inc=1,
                device_id=(partner(me, g, length),),
                device_id_type=pl.DeviceIdType.MESH,
            )

    loads = [pltpu.make_async_copy(given[k], held[k], load_sem.at[k]) for k in range(12)]
    for k in (7, 6, 4, 5, 3, 8, 9, 10, 2, 1, 0, 11):
        loads[k].start()

    depth = lax.rem(me, RING)

    def in_turn(send):
        @pl.when(depth < RING // 2)
        def _():
            send((7, 6, 5, 4, 3, 2, 1, 0))

        @pl.when(depth >= RING // 2)
        def _():
            send((3, 2, 1, 0, 7, 6, 5, 4))

    def start(copy, g):
        @pl.when(receives(g))
        def _():
            copy.start()

    def wait(copy, g):
        @pl.when(sends(g))
        def _():
            copy.wait_recv()

    def wait_sent(copy, g):
        @pl.when(receives(g))
        def _():
            copy.wait_send()

    def partial_copy(step, g):
        return pltpu.make_async_remote_copy(
            src_ref=leaving.at[pl.ds(SENT * g, SENT)],
            dst_ref=table.at[pl.ds(1 + OWN + SLOTS * g, SENT)],
            send_sem=send_sem.at[step, 0, g],
            recv_sem=recv_sem.at[step, 0, g],
            device_id=(partner(me, g, length),),
            device_id_type=pl.DeviceIdType.MESH,
        )

    def speed_copy(step, g):
        return pltpu.make_async_remote_copy(
            src_ref=speed_out.at[pl.ds(3 * g, 3)],
            dst_ref=speed_in.at[pl.ds(3 * g, 3)],
            send_sem=send_sem.at[step, 1, g],
            recv_sem=recv_sem.at[step, 1, g],
            device_id=(partner(me, g, length),),
            device_id_type=pl.DeviceIdType.MESH,
        )

    row_id = lax.broadcasted_iota(jnp.int32, (8, 128), 0)
    lane_id = lax.broadcasted_iota(jnp.int32, (8, 128), 1)
    upper = row_id < 4
    left = lane_id < 64
    diagonal = upper == left
    upper_left = upper & left
    lower_right = diagonal & ~upper
    channel = row_id % 4
    zero_tile = jnp.zeros((8, 128), jnp.float32)

    slot = lane_id + 128 * (row_id % 2)

    def live_slots(r):
        limit = counts[4 * r + 3]
        for k in (2, 1, 0):
            limit = jnp.where(row_id < 2 * k + 2, counts[4 * r + k], limit)
        return slot < limit

    ones = jnp.where((row_id == 0) | (row_id == 4), 1.0, 0.0)

    def load_tile(t, carry):
        lanes = pl.ds(pl.multiple_of(128 * t, 128), 128)
        spot = pl.ds(pl.multiple_of(8 * t, 8), 8)
        move[spot, :] = jnp.concatenate(
            [offset_in[:, lanes], velocity_in[:, lanes], zero_tile[0:2]], axis=0
        )
        affine8[spot, :] = affine_in[0:8, lanes]
        deform8[spot, :] = strain_in[0:8, lanes] + ones
        ninth[spot, :] = jnp.concatenate(
            [affine_in[8:9, lanes], strain_in[8:9, lanes] + 1.0, zero_tile[0:6]], axis=0
        )
        part_b[spot, :] = zero_tile
        part_c[spot, :] = zero_tile
        part_d[spot, :] = zero_tile
        spots_b[spot, :] = zero_tile
        return carry

    for k in (7, 6, 4, 5):
        loads[k].wait()
    lax.fori_loop(0, TILES, load_tile, 0, unroll=4)
    for k in (3, 8, 9, 10, 2):
        loads[k].wait()
    plastic[...] = plastic_in[...]
    table[0] = zero_tile
    padded[0] = zero_tile
    for g in range(GROUPS):

        @pl.when(jnp.logical_not(sends(g)))
        def _():
            for k in range(SENT):
                table[1 + OWN + SLOTS * g + k] = zero_tile
            for k in range(3):
                speed_in[3 * g + k] = zero_tile

    def one_step(step, carry):
        def particles(r, carry):
            band = pl.ds(pl.multiple_of(8 * r, 8), 8)

            def every(i):
                return pl.ds(64 * r + i, 8, stride=8)

            f = [deform8[every(k), :] for k in range(8)] + [ninth[every(1), :]]
            volume = determinant(f)
            clamped = jnp.clip(volume, 1.0 - COMPRESS, 1.0 + STRETCH)
            hardened = plastic[band, :] * volume / clamped
            factor = jnp.exp(jnp.log(clamped / volume) / 3.0)
            e = [x * factor for x in f]
            for k in range(9):
                elastic[k, band, :] = e[k]
            elastic[9, band, :] = hardened
            live = live_slots(r)
            mass = jnp.where(live, mass_in[band, :], 0.0)
            stiff = jnp.exp(HARDEN * (1.0 - hardened))
            shear = SHEAR * stiff
            bulk = BULK * stiff * jnp.log(clamped)
            part_a[every(0), :] = mass
            part_a[every(4), :] = mass
            for i in range(3):
                value = mass * move[every(3 + i), :]
                part_a[every(1 + i), :] = value
                part_a[every(5 + i), :] = value
            inner = {}
            for i in range(3):
                for j in range(i, 3):
                    total = (
                        e[3 * i] * e[3 * j]
                        + e[3 * i + 1] * e[3 * j + 1]
                        + e[3 * i + 2] * e[3 * j + 2]
                    )
                    stress = shear * (total - 1.0) + bulk if i == j else shear * total
                    inner[i, j] = inner[j, i] = stress
            for i in range(3):
                for j, target in enumerate((part_b, part_c, part_d)):
                    k = 3 * i + j
                    affine = affine8[every(k), :] if k < 8 else ninth[every(0), :]
                    value = mass * (affine - (4.0 * DT) * inner[i, j])
                    value = jnp.where(live, value, 0.0)
                    target[every(1 + i), :] = value
                    target[every(5 + i), :] = value
            cell = cells[band, :]
            corner = (cell >> 4, (cell >> 2) & 3, cell & 3)
            spots = []
            for i in range(3):
                c = corner[i].astype(jnp.float32)
                frac = 0.5 + move[every(i), :]
                spots += [
                    c,
                    c + frac,
                    0.5 * (1.5 - frac) * (1.5 - frac),
                    0.75 - (frac - 1.0) * (frac - 1.0),
                    0.5 * (frac - 0.5) * (frac - 0.5),
                ]
            for k, value in enumerate(spots):
                if k < 8:
                    spots_a[every(k), :] = value
                else:
                    spots_b[every(k - 8), :] = value
            return carry

        lax.fori_loop(0, TILES // 8, particles, 0)

        places = lax.broadcasted_iota(jnp.int32, (8, PMAX), 0).astype(jnp.float32)

        def spline_rows(spots):
            w = weight(places, spots)
            return w, w * (places - spots[1])

        def spread_rows(x, at, count):
            parts = []
            for k in range(0, count, 8):
                index = consts[at + k : at + k + 8, :]
                parts.append(
                    jnp.concatenate(
                        [jnp.take_along_axis(x[:, l : l + 128], index, axis=0) for l in (0, 128)],
                        axis=1,
                    )
                )
            return jnp.concatenate(parts, axis=0)

        def scatter(b, carry):
            mass_flow = pair(part_a, b)
            push = [pair(part_b, b), pair(part_c, b), pair(part_d, b)]
            tile_a = pair(spots_a, b)
            tile_b = pair(spots_b, b)
            lines = [tile_a[k : k + 1] for k in range(8)] + [tile_b[k : k + 1] for k in range(7)]
            first, second, third = lines[0:5], lines[5:10], lines[10:15]
            blocks = [[], [], []]
            weights = []
            first_pair = spline_rows(first)
            for a in range(3):
                w, d = (spread_rows(x, 80 + 8 * a, 8) for x in first_pair)
                weights.append((w, d))
                blocks[0].append(w * mass_flow + d * push[0])
                blocks[1].append(w * push[1])
                blocks[2].append(w * push[2])
            spot = pl.ds(pl.multiple_of(24 * b, 8), 24)
            first_w[spot, :] = jnp.concatenate([w for w, d in weights], axis=0)
            first_d[spot, :] = jnp.concatenate([d for w, d in weights], axis=0)
            lhs = jnp.concatenate([jnp.concatenate(x, axis=0) for x in blocks], axis=1)
            second_w, second_d = (spread_rows(x, 0, 40) for x in spline_rows(second))
            third_w, third_d = (spread_rows(x, 40, 40) for x in spline_rows(third))
            rhs = jnp.concatenate(
                [second_w * third_w, second_d * third_w, second_w * third_d], axis=1
            )
            rhs = jnp.concatenate([rhs, jnp.zeros((8, 3 * PMAX), jnp.float32)], axis=0)
            rhs = high_low(rhs, 0)
            products[pl.ds(pl.multiple_of(96 * b, 16), 96), :] = rhs
            lhs = high_low(lhs, 0)
            both = dot_nt(lhs, rhs[0:48]) + dot_nt(lhs, rhs[48:96])
            total = both[0:24] + both[24:48]
            block = jnp.concatenate(
                [
                    total[0:8, 0:36],
                    total[8:16, 0:RIM],
                    total[16:24, 0:RIM],
                    total[8:16, RIM:36],
                    total[16:24, RIM:36],
                    zero_tile[:, 0:20],
                ],
                axis=1,
            )
            own[b] = block
            table[1 + b] = block
            return carry

        lax.fori_loop(0, OWN, scatter, 0, unroll=16)

        @pl.when(step == 0)
        def _():
            for k in (1, 0, 11):
                loads[k].wait()
            pl.semaphore_wait(
                barrier, jnp.minimum(me, HOPS) + jnp.minimum(length - 1 - me, HOPS)
            )

        def send_partials(order):
            for g in order:
                tiles = [own[rows[0, SLOTS * g + k]] for k in range(SLOTS)]
                for m in range(SLOTS - SENT):
                    third = tiles[SENT + m]
                    for k, by in ((2 * m, USED), (2 * m + 1, 2 * USED - 128)):
                        leaving[SENT * g + k] = jnp.where(
                            lane_id < USED, tiles[k], pltpu.roll(third, by, 1)
                        )
                start(partial_copy(step, g), g)

        in_turn(send_partials)

        @pl.when(step == 1)
        def _():
            for g in FAR_FIRST:
                wait_sent(speed_copy(0, g), g)

        for g in NEAR_FIRST:
            wait(partial_copy(step, g), g)
        for g in range(GROUPS):
            at = 1 + OWN + SLOTS * g
            for m in range(SLOTS - SENT):
                table[at + SENT + m] = jnp.where(
                    lane_id < 128 - USED,
                    pltpu.roll(table[at + 2 * m], 128 - USED, 1),
                    pltpu.roll(table[at + 2 * m + 1], 256 - 2 * USED, 1),
                )

        offset_id = consts[104:112, :]

        def collect(o, total):
            here = offset_id == o
            return tuple(
                jnp.where(here, table[1 + links[b, o]], total[b]) for b in range(OWN)
            )

        total = tuple(own[b] for b in range(OWN))
        for o in OTHERS:
            total = collect(o, total)
        total = dot_nn(high_low(jnp.concatenate(total, axis=0), 1), fold_mats[0])
        for b in range(OWN):
            node = total[8 * b : 8 * b + 8]
            node = node + pltpu.roll(pltpu.roll(node, 4, 0), 64, 1)
            node = jnp.where(diagonal, node, 0.0)
            mass = jnp.where(channel == 0, node, 0.0)
            mass = mass + pltpu.roll(mass, 1, 0)
            mass = mass + pltpu.roll(mass, 2, 0)
            node = node / jnp.maximum(mass, MASS_FLOOR)
            node = node - jnp.where(channel == 3, DT * GRAVITY, 0.0)
            node = jnp.where(diagonal, node, 0.0)
            speed[b] = node
            speed_side[b] = pltpu.roll(node, 64, 1)

        def send_speeds(order):
            for g in order:
                for m in range(3):
                    r = [rows[0, SLOTS * g + 4 * m + k] for k in range(4)]
                    speed_out[3 * g + m] = jnp.where(
                        upper, speed[r[0]], speed[r[1]]
                    ) + jnp.where(upper, speed_side[r[2]], speed_side[r[3]])
                start(speed_copy(step, g), g)

        in_turn(send_speeds)
        for g in FAR_FIRST:
            wait_sent(partial_copy(step, g), g)

        def spread(tiles):
            x = high_low(jnp.concatenate(tiles, axis=0), 1)
            return dot_nn(x, fold_mats[1]).reshape(len(tiles), 8, 128)

        padded[1 : 1 + OWN] = spread([speed[b] for b in range(OWN)])
        for batch in (NEAR_FIRST[0:4], NEAR_FIRST[4:8]):
            for g in batch:
                wait(speed_copy(step, g), g)
            tiles = []
            for g in batch:
                for m in range(3):
                    z = speed_in[3 * g + m]
                    zs = pltpu.roll(z, 4, 0)
                    zl = pltpu.roll(z, 64, 1)
                    zd = pltpu.roll(zs, 64, 1)
                    tiles.append(jnp.where(upper_left, z, jnp.where(lower_right, zd, 0.0)))
                    tiles.append(jnp.where(upper_left, zd, jnp.where(lower_right, z, 0.0)))
                    tiles.append(jnp.where(upper_left, zl, jnp.where(lower_right, zs, 0.0)))
                    tiles.append(jnp.where(upper_left, zs, jnp.where(lower_right, zl, 0.0)))
            tiles = spread(tiles)
            for k, g in enumerate(batch):
                at = 1 + OWN + SLOTS * g
                padded[at : at + SLOTS] = tiles[SLOTS * k : SLOTS * (k + 1)]

        def fetch(o, total):
            here = offset_id == 26 - o
            return tuple(
                jnp.where(here, padded[1 + links[b, o]], total[b]) for b in range(OWN)
            )

        total = tuple(padded[1 + b] for b in range(OWN))
        for o in OTHERS:
            total = fetch(o, total)
        for b in range(OWN):
            field[b] = total[b]

        upper_wide = lax.broadcasted_iota(jnp.int32, (8, PMAX), 0) < 4

        def gather(b, carry):
            v = field[b]
            fill = zero_tile[:, 0:12]
            v = jnp.concatenate(
                [
                    jnp.concatenate([v[:, 0:36], fill], axis=1),
                    jnp.concatenate([v[:, 36:56], v[:, 76:92], fill], axis=1),
                    jnp.concatenate([v[:, 56:76], v[:, 92:108], fill], axis=1),
                ],
                axis=0,
            )
            v = high_low(jnp.concatenate([v, v], axis=1), 0)
            both = dot_nn(v, products[pl.ds(pl.multiple_of(96 * b, 16), 96), :])
            result = both[0:24] + both[24:48]
            spot = pl.ds(pl.multiple_of(24 * b, 8), 24)

            def fold(x):
                x = x[0:8] + x[8:16] + x[16:24]
                return x + pltpu.roll(x, 4, 0)

            w = first_w[spot, :]
            plain = fold(w * result[:, 0:PMAX])
            by1 = fold(first_d[spot, :] * result[:, 0:PMAX])
            by2 = fold(w * result[:, PMAX : 2 * PMAX])
            by3 = fold(w * result[:, 2 * PMAX : 3 * PMAX])
            spot = pl.ds(pl.multiple_of(16 * b, 16), 16)
            out = jnp.where(upper_wide, plain, by1)
            found_a[spot, :] = jnp.concatenate([out[:, 0:128], out[:, 128:256]], axis=0)
            out = jnp.where(upper_wide, by2, by3)
            found_b[spot, :] = jnp.concatenate([out[:, 0:128], out[:, 128:256]], axis=0)
            return carry

        lax.fori_loop(0, OWN, gather, 0, unroll=16)

        def finish(r, carry):
            band = pl.ds(pl.multiple_of(8 * r, 8), 8)

            def every(i):
                return pl.ds(64 * r + i, 8, stride=8)

            live = live_slots(r)

            def put(ref, i, value):
                ref[every(i), :] = jnp.where(live, value, ref[every(i), :])

            v = [found_a[every(1 + i), :] for i in range(3)]
            moment = [
                [found_a[every(5 + i), :] for i in range(3)],
                [found_b[every(1 + i), :] for i in range(3)],
                [found_b[every(5 + i), :] for i in range(3)],
            ]
            affine = [4.0 * moment[j][i] for i in range(3) for j in range(3)]
            e = [elastic[k, band, :] for k in range(9)]
            for i in range(3):
                put(move, i, move[every(i), :] + DT * v[i])
                put(move, 3 + i, v[i])
            for i in range(3):
                for j in range(3):
                    k = 3 * i + j
                    total = e[k]
                    for m in range(3):
                        total = total + DT * affine[3 * i + m] * e[3 * m + j]
                    if k < 8:
                        put(affine8, k, affine[k])
                        put(deform8, k, total)
                    else:
                        put(ninth, 0, affine[k])
                        put(ninth, 1, total)
            plastic[band, :] = jnp.where(live, elastic[9, band, :], plastic[band, :])
            return carry

        lax.fori_loop(0, TILES // 8, finish, 0)
        return carry

    lax.fori_loop(0, 2, one_step, 0)
    for g in FAR_FIRST:
        wait_sent(speed_copy(1, g), g)

    def store_tile(t, carry):
        lanes = pl.ds(pl.multiple_of(128 * t, 128), 128)
        spot = pl.ds(pl.multiple_of(8 * t, 8), 8)
        value = move[spot, :]
        offset_out[:, lanes] = value[0:3]
        velocity_out[:, lanes] = value[3:6]
        affine_out[0:8, lanes] = affine8[spot, :]
        deform_out[0:8, lanes] = deform8[spot, :]
        value = ninth[spot, :]
        affine_out[8:9, lanes] = value[0:1]
        deform_out[8:9, lanes] = value[1:2]
        return carry

    lax.fori_loop(0, TILES, store_tile, 0, unroll=4)


def hand_over(*refs):
    first, last, held = refs[0:5], refs[5:10], refs[10:15]
    copies = []
    for k in range(5):
        come = pltpu.make_async_copy(first[k], held[k], refs[15].at[0, k])
        leave = pltpu.make_async_copy(held[k], last[k], refs[15].at[1, k])
        copies.append((come, leave))
        come.start()
    for come, leave in copies:
        come.wait()
        leave.start()
    for come, leave in copies:
        leave.wait()


def on_device(
    length,
    base_cell,
    offset,
    velocity,
    affine,
    strain,
    plastic,
    particle_mass,
    counts,
    neighbours,
    send_rows,
):
    consts, folds = tables()
    hbm = pl.BlockSpec(memory_space=pltpu.HBM)
    vmem = pl.BlockSpec(memory_space=pltpu.VMEM)
    f32 = jnp.float32
    i32 = jnp.int32
    tile = pltpu.VMEM((8 * TILES, 128), f32)
    planar = (TILES, 128)
    row3 = (3, PARTICLES)
    row9 = (9, PARTICLES)
    shapes = [jax.ShapeDtypeStruct(x, f32) for x in (row3, row3, row9, row9, planar)]
    outs = pl.pallas_call(
        lambda *refs: step_kernel(length, *refs),
        out_shape=shapes,
        in_specs=[hbm] * 12,
        out_specs=[vmem] * 5,
        scratch_shapes=[
            pltpu.SMEM((OWN, 27), i32),
            pltpu.SMEM((1, RECEIVED), i32),
            pltpu.SMEM((OWN,), i32),
            pltpu.VMEM(planar, i32),
            pltpu.VMEM(row3, f32),
            pltpu.VMEM(row3, f32),
            pltpu.VMEM(row9, f32),
            pltpu.VMEM(row9, f32),
            pltpu.VMEM(planar, f32),
            pltpu.VMEM(planar, f32),
            pltpu.VMEM((112, 128), i32),
            pltpu.VMEM((2, 256, 128), jnp.bfloat16),
            tile,
            tile,
            tile,
            tile,
            pltpu.VMEM((10,) + planar, f32),
            tile,
            tile,
            tile,
            tile,
            tile,
            tile,
            pltpu.VMEM((96 * OWN, 3 * PMAX), jnp.bfloat16),
            pltpu.VMEM((24 * OWN, PMAX), f32),
            pltpu.VMEM((24 * OWN, PMAX), f32),
            pltpu.VMEM((OWN, 8, 128), f32),
            pltpu.VMEM((TABLE, 8, 128), f32),
            pltpu.VMEM((SENT * GROUPS, 8, 128), f32),
            pltpu.VMEM((OWN, 8, 128), f32),
            pltpu.VMEM((OWN, 8, 128), f32),
            pltpu.VMEM((3 * GROUPS, 8, 128), f32),
            pltpu.VMEM((3 * GROUPS, 8, 128), f32),
            pltpu.VMEM((TABLE, 8, 128), f32),
            pltpu.VMEM((OWN, 8, 128), f32),
            tile,
            tile,
            pltpu.SemaphoreType.DMA((2, 2, GROUPS)),
            pltpu.SemaphoreType.DMA((2, 2, GROUPS)),
            pltpu.SemaphoreType.DMA((12,)),
        ],
        compiler_params=pltpu.CompilerParams(
            collective_id=0, has_side_effects=True, vmem_limit_bytes=62 * 1024 * 1024
        ),
        name="snow_steps",
    )(
        neighbours,
        send_rows,
        counts,
        base_cell.reshape(planar),
        offset,
        velocity,
        affine,
        strain,
        plastic.reshape(planar),
        particle_mass.reshape(planar),
        jnp.asarray(consts),
        jnp.asarray(folds, dtype=jnp.bfloat16),
    )
    outs = pl.pallas_call(
        hand_over,
        out_shape=shapes,
        in_specs=[hbm] * 5,
        out_specs=[hbm] * 5,
        scratch_shapes=[pltpu.VMEM(x.shape, f32) for x in shapes] + [pltpu.SemaphoreType.DMA((2, 5))],
        compiler_params=pltpu.CompilerParams(vmem_limit_bytes=62 * 1024 * 1024),
        name="hand_over",
    )(*outs)
    return tuple(outs[:4]) + (outs[4].reshape(PARTICLES),)


def solution(mesh):
    length = mesh.shape["dom"]
    wide = P(None, "dom")
    flat = P("dom")
    return jax.shard_map(
        lambda *args: on_device(length, *args),
        mesh=mesh,
        in_specs=(flat, wide, wide, wide, wide, flat, flat, flat, P("dom", None), P("dom", None)),
        out_specs=(wide, wide, wide, wide, flat),
        check_vma=False,
    )
```

```python
import jax
import jax.numpy as jnp
import numpy as np
from jax import lax
from jax.experimental import pallas as pl
from jax.experimental.pallas import tpu as pltpu
from jax.sharding import PartitionSpec as P

OWN = 16
PMAX = 256
HOPS = 4
SLOTS = 12
GROUPS = 2 * HOPS
RECEIVED = GROUPS * SLOTS
TABLE = 1 + OWN + RECEIVED
PARTICLES = OWN * PMAX
TILES = PARTICLES // 128
RIM = 20
USED = 36 + 2 * RIM
SENT = 8
RING = 16
OTHERS = tuple(o for o in range(27) if o != 13)
FAR_FIRST = (3, 7, 2, 6, 1, 5, 0, 4)
NEAR_FIRST = (0, 4, 1, 5, 2, 6, 3, 7)

DT = 0.05
SHEAR = 4.0
BULK = 4.0
HARDEN = 10.0
COMPRESS = 0.025
STRETCH = 0.0075
GRAVITY = 1.0
MASS_FLOOR = 0.25


def tables():
    places = [(j2, j3) for j2 in range(6) for j3 in range(6)]
    places.sort(key=lambda x: (x[0] in (1, 2, 3, 4) and x[1] in (1, 2, 3, 4), x))
    lanes = [(0, q) for q in range(36)]
    lanes += [(a, q) for a in (1, 2) for q in range(RIM)]
    lanes += [(a, q) for a in (1, 2) for q in range(RIM, 36)]
    lanes += [(3, 0)] * 20
    half = np.arange(8)[:, None] // 4 + np.zeros((1, 128), int)
    third = np.array([x[0] for x in lanes])[None, :] + 0 * half
    place = np.array([x[1] for x in lanes])[None, :] + 0 * half
    inside = third < 3
    spot2 = np.array([x[0] for x in places])
    spot3 = np.array([x[1] for x in places])
    node = [np.where(half == 0, third, 5 - third), spot2[place], spot3[place]]
    step = [(x == 0).astype(int) - (x == 5).astype(int) for x in node]
    offset_id = 9 * (step[0] + 1) + 3 * (step[1] + 1) + step[2] + 1
    offset_id = np.where(inside, offset_id, 13)
    core = [(x + 3) % 4 for x in node]
    core_id = np.where(inside, 16 * core[0] + 4 * core[1] + core[2], -1)
    fold = np.zeros((128, 128), np.float32)
    for h in range(2):
        for l in range(108):
            fold[l, 64 * h + core_id[4 * h, l]] = 1.0
    wide = np.zeros((40, 128))
    none = [6] * 4
    consts = np.concatenate(
        [
            wide + np.append(spot2, none)[:, None],
            wide + np.append(spot3, none)[:, None],
            np.where(half == 0, 0, 5),
            np.where(half == 0, 1, 4),
            np.where(half == 0, 2, 3),
            offset_id,
        ]
    ).astype(np.int32)
    folds = np.stack([np.concatenate([fold, fold]), np.concatenate([fold.T, fold.T])])
    return consts, folds


def determinant(m):
    return (
        m[0] * (m[4] * m[8] - m[5] * m[7])
        - m[1] * (m[3] * m[8] - m[5] * m[6])
        + m[2] * (m[3] * m[7] - m[4] * m[6])
    )


def low_part(x):
    return x - x.astype(jnp.bfloat16).astype(jnp.float32)


def high_low(x, axis):
    return jnp.concatenate([x, low_part(x)], axis=axis).astype(jnp.bfloat16)


def dot_nt(a, b):
    return lax.dot_general(a, b, (((1,), (1,)), ((), ())), preferred_element_type=jnp.float32)


def dot_nn(a, b):
    return lax.dot_general(a, b, (((1,), (0,)), ((), ())), preferred_element_type=jnp.float32)


def weight(node, spots):
    cell, _, first, second, third = spots
    shift = node - cell
    value = jnp.where(shift == 2.0, third, 0.0)
    value = jnp.where(shift == 1.0, second, value)
    return jnp.where(shift == 0.0, first, value)


def pair(ref, b):
    both = ref[pl.ds(pl.multiple_of(16 * b, 16), 16), :]
    return jnp.concatenate([both[0:8], both[8:16]], axis=1)


def reach(group):
    return group + 1 if group < HOPS else -(group - HOPS + 1)


def partner(me, group, length):
    return lax.rem(me + (reach(group) + length), length)


def step_kernel(length, *refs):
    given, results, held, work = refs[0:12], refs[12:17], refs[17:29], refs[29:]
    (
        links,
        rows,
        counts,
        cells,
        offset_in,
        velocity_in,
        affine_in,
        strain_in,
        plastic_in,
        mass_in,
        consts,
        fold_mats,
    ) = held
    offset_out, velocity_out, affine_out, deform_out, plastic = results
    (
        move,
        affine8,
        deform8,
        ninth,
        elastic,
        part_a,
        part_b,
        part_c,
        part_d,
        spots_a,
        spots_b,
        products,
        first_w,
        first_d,
        own,
        table,
        leaving,
        speed,
        speed_side,
        speed_out,
        speed_in,
        padded,
        field,
        found_a,
        found_b,
        send_sem,
        recv_sem,
        load_sem,
    ) = work
    me = lax.axis_index("dom")
    barrier = pltpu.get_barrier_semaphore()

    def receives(g):
        return (me + reach(g) >= 0) & (me + reach(g) < length)

    def sends(g):
        return (me - reach(g) >= 0) & (me - reach(g) < length)

    for g in range(GROUPS):

        @pl.when(receives(g))
        def _():
            pl.semaphore_signal(
                barrier,
                inc=1,
                device_id=(partner(me, g, length),),
                device_id_type=pl.DeviceIdType.MESH,
            )

    loads = [pltpu.make_async_copy(given[k], held[k], load_sem.at[k]) for k in range(12)]
    for k in (7, 6, 4, 5, 3, 8, 9, 10, 2, 1, 0, 11):
        loads[k].start()

    depth = lax.rem(me, RING)

    def in_turn(send):
        @pl.when(depth < RING // 2)
        def _():
            send((7, 6, 5, 4, 3, 2, 1, 0))

        @pl.when(depth >= RING // 2)
        def _():
            send((3, 2, 1, 0, 7, 6, 5, 4))

    def start(copy, g):
        @pl.when(receives(g))
        def _():
            copy.start()

    def wait(copy, g):
        @pl.when(sends(g))
        def _():
            copy.wait_recv()

    def wait_sent(copy, g):
        @pl.when(receives(g))
        def _():
            copy.wait_send()

    def partial_copy(step, g):
        return pltpu.make_async_remote_copy(
            src_ref=leaving.at[pl.ds(SENT * g, SENT)],
            dst_ref=table.at[pl.ds(1 + OWN + SLOTS * g, SENT)],
            send_sem=send_sem.at[step, 0, g],
            recv_sem=recv_sem.at[step, 0, g],
            device_id=(partner(me, g, length),),
            device_id_type=pl.DeviceIdType.MESH,
        )

    def speed_copy(step, g):
        return pltpu.make_async_remote_copy(
            src_ref=speed_out.at[pl.ds(3 * g, 3)],
            dst_ref=speed_in.at[pl.ds(3 * g, 3)],
            send_sem=send_sem.at[step, 1, g],
            recv_sem=recv_sem.at[step, 1, g],
            device_id=(partner(me, g, length),),
            device_id_type=pl.DeviceIdType.MESH,
        )

    row_id = lax.broadcasted_iota(jnp.int32, (8, 128), 0)
    lane_id = lax.broadcasted_iota(jnp.int32, (8, 128), 1)
    upper = row_id < 4
    left = lane_id < 64
    diagonal = upper == left
    upper_left = upper & left
    lower_right = diagonal & ~upper
    channel = row_id % 4
    zero_tile = jnp.zeros((8, 128), jnp.float32)

    slot = lane_id + 128 * (row_id % 2)

    def live_slots(r):
        limit = counts[4 * r + 3]
        for k in (2, 1, 0):
            limit = jnp.where(row_id < 2 * k + 2, counts[4 * r + k], limit)
        return slot < limit

    ones = jnp.where((row_id == 0) | (row_id == 4), 1.0, 0.0)

    def load_tile(t, carry):
        lanes = pl.ds(pl.multiple_of(128 * t, 128), 128)
        spot = pl.ds(pl.multiple_of(8 * t, 8), 8)
        move[spot, :] = jnp.concatenate(
            [offset_in[:, lanes], velocity_in[:, lanes], zero_tile[0:2]], axis=0
        )
        affine8[spot, :] = affine_in[0:8, lanes]
        deform8[spot, :] = strain_in[0:8, lanes] + ones
        ninth[spot, :] = jnp.concatenate(
            [affine_in[8:9, lanes], strain_in[8:9, lanes] + 1.0, zero_tile[0:6]], axis=0
        )
        part_b[spot, :] = zero_tile
        part_c[spot, :] = zero_tile
        part_d[spot, :] = zero_tile
        spots_b[spot, :] = zero_tile
        return carry

    for k in (7, 6, 4, 5):
        loads[k].wait()
    lax.fori_loop(0, TILES, load_tile, 0, unroll=4)
    for k in (3, 8, 9, 10, 2):
        loads[k].wait()
    plastic[...] = plastic_in[...]
    table[0] = zero_tile
    padded[0] = zero_tile
    for g in range(GROUPS):

        @pl.when(jnp.logical_not(sends(g)))
        def _():
            for k in range(SENT):
                table[1 + OWN + SLOTS * g + k] = zero_tile
            for k in range(3):
                speed_in[3 * g + k] = zero_tile

    def one_step(step, carry):
        def particles(r, carry):
            band = pl.ds(pl.multiple_of(8 * r, 8), 8)

            def every(i):
                return pl.ds(64 * r + i, 8, stride=8)

            f = [deform8[every(k), :] for k in range(8)] + [ninth[every(1), :]]
            volume = determinant(f)
            clamped = jnp.clip(volume, 1.0 - COMPRESS, 1.0 + STRETCH)
            hardened = plastic[band, :] * volume / clamped
            factor = jnp.exp(jnp.log(clamped / volume) / 3.0)
            e = [x * factor for x in f]
            for k in range(9):
                elastic[k, band, :] = e[k]
            elastic[9, band, :] = hardened
            live = live_slots(r)
            mass = jnp.where(live, mass_in[band, :], 0.0)
            stiff = jnp.exp(HARDEN * (1.0 - hardened))
            shear = SHEAR * stiff
            bulk = BULK * stiff * jnp.log(clamped)
            part_a[every(0), :] = mass
            part_a[every(4), :] = mass
            for i in range(3):
                value = mass * move[every(3 + i), :]
                part_a[every(1 + i), :] = value
                part_a[every(5 + i), :] = value
            inner = {}
            for i in range(3):
                for j in range(i, 3):
                    total = (
                        e[3 * i] * e[3 * j]
                        + e[3 * i + 1] * e[3 * j + 1]
                        + e[3 * i + 2] * e[3 * j + 2]
                    )
                    stress = shear * (total - 1.0) + bulk if i == j else shear * total
                    inner[i, j] = inner[j, i] = stress
            for i in range(3):
                for j, target in enumerate((part_b, part_c, part_d)):
                    k = 3 * i + j
                    affine = affine8[every(k), :] if k < 8 else ninth[every(0), :]
                    value = mass * (affine - (4.0 * DT) * inner[i, j])
                    value = jnp.where(live, value, 0.0)
                    target[every(1 + i), :] = value
                    target[every(5 + i), :] = value
            cell = cells[band, :]
            corner = (cell >> 4, (cell >> 2) & 3, cell & 3)
            spots = []
            for i in range(3):
                c = corner[i].astype(jnp.float32)
                frac = 0.5 + move[every(i), :]
                spots += [
                    c,
                    c + frac,
                    0.5 * (1.5 - frac) * (1.5 - frac),
                    0.75 - (frac - 1.0) * (frac - 1.0),
                    0.5 * (frac - 0.5) * (frac - 0.5),
                ]
            for k, value in enumerate(spots):
                if k < 8:
                    spots_a[every(k), :] = value
                else:
                    spots_b[every(k - 8), :] = value
            return carry

        lax.fori_loop(0, TILES // 8, particles, 0)

        places = lax.broadcasted_iota(jnp.int32, (8, PMAX), 0).astype(jnp.float32)

        def spline_rows(spots):
            w = weight(places, spots)
            return w, w * (places - spots[1])

        def spread_rows(x, at, count):
            parts = []
            for k in range(0, count, 8):
                index = consts[at + k : at + k + 8, :]
                parts.append(
                    jnp.concatenate(
                        [jnp.take_along_axis(x[:, l : l + 128], index, axis=0) for l in (0, 128)],
                        axis=1,
                    )
                )
            return jnp.concatenate(parts, axis=0)

        def scatter(b, carry):
            mass_flow = pair(part_a, b)
            push = [pair(part_b, b), pair(part_c, b), pair(part_d, b)]
            tile_a = pair(spots_a, b)
            tile_b = pair(spots_b, b)
            lines = [tile_a[k : k + 1] for k in range(8)] + [tile_b[k : k + 1] for k in range(7)]
            first, second, third = lines[0:5], lines[5:10], lines[10:15]
            blocks = [[], [], []]
            weights = []
            first_pair = spline_rows(first)
            for a in range(3):
                w, d = (spread_rows(x, 80 + 8 * a, 8) for x in first_pair)
                weights.append((w, d))
                blocks[0].append(w * mass_flow + d * push[0])
                blocks[1].append(w * push[1])
                blocks[2].append(w * push[2])
            spot = pl.ds(pl.multiple_of(24 * b, 8), 24)
            first_w[spot, :] = jnp.concatenate([w for w, d in weights], axis=0)
            first_d[spot, :] = jnp.concatenate([d for w, d in weights], axis=0)
            lhs = jnp.concatenate([jnp.concatenate(x, axis=0) for x in blocks], axis=1)
            second_w, second_d = (spread_rows(x, 0, 40) for x in spline_rows(second))
            third_w, third_d = (spread_rows(x, 40, 40) for x in spline_rows(third))
            rhs = jnp.concatenate(
                [second_w * third_w, second_d * third_w, second_w * third_d], axis=1
            )
            rhs = jnp.concatenate([rhs, jnp.zeros((8, 3 * PMAX), jnp.float32)], axis=0)
            rhs = high_low(rhs, 0)
            products[pl.ds(pl.multiple_of(96 * b, 16), 96), :] = rhs
            lhs = high_low(lhs, 0)
            both = dot_nt(lhs, rhs[0:48]) + dot_nt(lhs, rhs[48:96])
            total = both[0:24] + both[24:48]
            block = jnp.concatenate(
                [
                    total[0:8, 0:36],
                    total[8:16, 0:RIM],
                    total[16:24, 0:RIM],
                    total[8:16, RIM:36],
                    total[16:24, RIM:36],
                    zero_tile[:, 0:20],
                ],
                axis=1,
            )
            own[b] = block
            table[1 + b] = block
            return carry

        lax.fori_loop(0, OWN, scatter, 0, unroll=16)

        @pl.when(step == 0)
        def _():
            for k in (1, 0, 11):
                loads[k].wait()
            pl.semaphore_wait(
                barrier, jnp.minimum(me, HOPS) + jnp.minimum(length - 1 - me, HOPS)
            )

        def send_partials(order):
            for g in order:
                tiles = [own[rows[0, SLOTS * g + k]] for k in range(SLOTS)]
                for m in range(SLOTS - SENT):
                    third = tiles[SENT + m]
                    for k, by in ((2 * m, USED), (2 * m + 1, 2 * USED - 128)):
                        leaving[SENT * g + k] = jnp.where(
                            lane_id < USED, tiles[k], pltpu.roll(third, by, 1)
                        )
                start(partial_copy(step, g), g)

        in_turn(send_partials)

        @pl.when(step == 1)
        def _():
            for g in FAR_FIRST:
                wait_sent(speed_copy(0, g), g)

        for g in NEAR_FIRST:
            wait(partial_copy(step, g), g)
        for g in range(GROUPS):
            at = 1 + OWN + SLOTS * g
            for m in range(SLOTS - SENT):
                table[at + SENT + m] = jnp.where(
                    lane_id < 128 - USED,
                    pltpu.roll(table[at + 2 * m], 128 - USED, 1),
                    pltpu.roll(table[at + 2 * m + 1], 256 - 2 * USED, 1),
                )

        offset_id = consts[104:112, :]

        def collect(o, total):
            here = offset_id == o
            return tuple(
                jnp.where(here, table[1 + links[b, o]], total[b]) for b in range(OWN)
            )

        total = tuple(own[b] for b in range(OWN))
        for o in OTHERS:
            total = collect(o, total)
        total = dot_nn(high_low(jnp.concatenate(total, axis=0), 1), fold_mats[0])
        for b in range(OWN):
            node = total[8 * b : 8 * b + 8]
            node = node + pltpu.roll(pltpu.roll(node, 4, 0), 64, 1)
            node = jnp.where(diagonal, node, 0.0)
            mass = jnp.where(channel == 0, node, 0.0)
            mass = mass + pltpu.roll(mass, 1, 0)
            mass = mass + pltpu.roll(mass, 2, 0)
            node = node / jnp.maximum(mass, MASS_FLOOR)
            node = node - jnp.where(channel == 3, DT * GRAVITY, 0.0)
            node = jnp.where(diagonal, node, 0.0)
            speed[b] = node
            speed_side[b] = pltpu.roll(node, 64, 1)

        def send_speeds(order):
            for g in order:
                for m in range(3):
                    r = [rows[0, SLOTS * g + 4 * m + k] for k in range(4)]
                    speed_out[3 * g + m] = jnp.where(
                        upper, speed[r[0]], speed[r[1]]
                    ) + jnp.where(upper, speed_side[r[2]], speed_side[r[3]])
                start(speed_copy(step, g), g)

        in_turn(send_speeds)
        for g in FAR_FIRST:
            wait_sent(partial_copy(step, g), g)

        def spread(tiles):
            x = high_low(jnp.concatenate(tiles, axis=0), 1)
            return dot_nn(x, fold_mats[1]).reshape(len(tiles), 8, 128)

        padded[1 : 1 + OWN] = spread([speed[b] for b in range(OWN)])
        for batch in (NEAR_FIRST[0:6], NEAR_FIRST[6:8]):
            for g in batch:
                wait(speed_copy(step, g), g)
            tiles = []
            for g in batch:
                for m in range(3):
                    z = speed_in[3 * g + m]
                    zs = pltpu.roll(z, 4, 0)
                    zl = pltpu.roll(z, 64, 1)
                    zd = pltpu.roll(zs, 64, 1)
                    tiles.append(jnp.where(upper_left, z, jnp.where(lower_right, zd, 0.0)))
                    tiles.append(jnp.where(upper_left, zd, jnp.where(lower_right, z, 0.0)))
                    tiles.append(jnp.where(upper_left, zl, jnp.where(lower_right, zs, 0.0)))
                    tiles.append(jnp.where(upper_left, zs, jnp.where(lower_right, zl, 0.0)))
            tiles = spread(tiles)
            for k, g in enumerate(batch):
                at = 1 + OWN + SLOTS * g
                padded[at : at + SLOTS] = tiles[SLOTS * k : SLOTS * (k + 1)]

        def fetch(o, total):
            here = offset_id == 26 - o
            return tuple(
                jnp.where(here, padded[1 + links[b, o]], total[b]) for b in range(OWN)
            )

        total = tuple(padded[1 + b] for b in range(OWN))
        for o in OTHERS:
            total = fetch(o, total)
        for b in range(OWN):
            field[b] = total[b]

        upper_wide = lax.broadcasted_iota(jnp.int32, (8, PMAX), 0) < 4

        def gather(b, carry):
            v = field[b]
            fill = zero_tile[:, 0:12]
            v = jnp.concatenate(
                [
                    jnp.concatenate([v[:, 0:36], fill], axis=1),
                    jnp.concatenate([v[:, 36:56], v[:, 76:92], fill], axis=1),
                    jnp.concatenate([v[:, 56:76], v[:, 92:108], fill], axis=1),
                ],
                axis=0,
            )
            v = high_low(jnp.concatenate([v, v], axis=1), 0)
            both = dot_nn(v, products[pl.ds(pl.multiple_of(96 * b, 16), 96), :])
            result = both[0:24] + both[24:48]
            spot = pl.ds(pl.multiple_of(24 * b, 8), 24)

            def fold(x):
                x = x[0:8] + x[8:16] + x[16:24]
                return x + pltpu.roll(x, 4, 0)

            w = first_w[spot, :]
            plain = fold(w * result[:, 0:PMAX])
            by1 = fold(first_d[spot, :] * result[:, 0:PMAX])
            by2 = fold(w * result[:, PMAX : 2 * PMAX])
            by3 = fold(w * result[:, 2 * PMAX : 3 * PMAX])
            spot = pl.ds(pl.multiple_of(16 * b, 16), 16)
            out = jnp.where(upper_wide, plain, by1)
            found_a[spot, :] = jnp.concatenate([out[:, 0:128], out[:, 128:256]], axis=0)
            out = jnp.where(upper_wide, by2, by3)
            found_b[spot, :] = jnp.concatenate([out[:, 0:128], out[:, 128:256]], axis=0)
            return carry

        lax.fori_loop(0, OWN, gather, 0, unroll=16)

        def finish(r, carry):
            band = pl.ds(pl.multiple_of(8 * r, 8), 8)

            def every(i):
                return pl.ds(64 * r + i, 8, stride=8)

            live = live_slots(r)

            def put(ref, i, value):
                ref[every(i), :] = jnp.where(live, value, ref[every(i), :])

            v = [found_a[every(1 + i), :] for i in range(3)]
            moment = [
                [found_a[every(5 + i), :] for i in range(3)],
                [found_b[every(1 + i), :] for i in range(3)],
                [found_b[every(5 + i), :] for i in range(3)],
            ]
            affine = [4.0 * moment[j][i] for i in range(3) for j in range(3)]
            e = [elastic[k, band, :] for k in range(9)]
            for i in range(3):
                put(move, i, move[every(i), :] + DT * v[i])
                put(move, 3 + i, v[i])
            for i in range(3):
                for j in range(3):
                    k = 3 * i + j
                    total = e[k]
                    for m in range(3):
                        total = total + DT * affine[3 * i + m] * e[3 * m + j]
                    if k < 8:
                        put(affine8, k, affine[k])
                        put(deform8, k, total)
                    else:
                        put(ninth, 0, affine[k])
                        put(ninth, 1, total)
            plastic[band, :] = jnp.where(live, elastic[9, band, :], plastic[band, :])
            return carry

        lax.fori_loop(0, TILES // 8, finish, 0)
        return carry

    lax.fori_loop(0, 2, one_step, 0)
    for g in FAR_FIRST:
        wait_sent(speed_copy(1, g), g)

    def store_tile(t, carry):
        lanes = pl.ds(pl.multiple_of(128 * t, 128), 128)
        spot = pl.ds(pl.multiple_of(8 * t, 8), 8)
        value = move[spot, :]
        offset_out[:, lanes] = value[0:3]
        velocity_out[:, lanes] = value[3:6]
        affine_out[0:8, lanes] = affine8[spot, :]
        deform_out[0:8, lanes] = deform8[spot, :]
        value = ninth[spot, :]
        affine_out[8:9, lanes] = value[0:1]
        deform_out[8:9, lanes] = value[1:2]
        return carry

    lax.fori_loop(0, TILES, store_tile, 0, unroll=4)


def hand_over(*refs):
    first, last, held = refs[0:5], refs[5:10], refs[10:15]
    copies = []
    for k in range(5):
        come = pltpu.make_async_copy(first[k], held[k], refs[15].at[0, k])
        leave = pltpu.make_async_copy(held[k], last[k], refs[15].at[1, k])
        copies.append((come, leave))
        come.start()
    for come, leave in copies:
        come.wait()
        leave.start()
    for come, leave in copies:
        leave.wait()


def on_device(
    length,
    base_cell,
    offset,
    velocity,
    affine,
    strain,
    plastic,
    particle_mass,
    counts,
    neighbours,
    send_rows,
):
    consts, folds = tables()
    hbm = pl.BlockSpec(memory_space=pltpu.HBM)
    vmem = pl.BlockSpec(memory_space=pltpu.VMEM)
    f32 = jnp.float32
    i32 = jnp.int32
    tile = pltpu.VMEM((8 * TILES, 128), f32)
    planar = (TILES, 128)
    row3 = (3, PARTICLES)
    row9 = (9, PARTICLES)
    shapes = [jax.ShapeDtypeStruct(x, f32) for x in (row3, row3, row9, row9, planar)]
    outs = pl.pallas_call(
        lambda *refs: step_kernel(length, *refs),
        out_shape=shapes,
        in_specs=[hbm] * 12,
        out_specs=[vmem] * 5,
        scratch_shapes=[
            pltpu.SMEM((OWN, 27), i32),
            pltpu.SMEM((1, RECEIVED), i32),
            pltpu.SMEM((OWN,), i32),
            pltpu.VMEM(planar, i32),
            pltpu.VMEM(row3, f32),
            pltpu.VMEM(row3, f32),
            pltpu.VMEM(row9, f32),
            pltpu.VMEM(row9, f32),
            pltpu.VMEM(planar, f32),
            pltpu.VMEM(planar, f32),
            pltpu.VMEM((112, 128), i32),
            pltpu.VMEM((2, 256, 128), jnp.bfloat16),
            tile,
            tile,
            tile,
            tile,
            pltpu.VMEM((10,) + planar, f32),
            tile,
            tile,
            tile,
            tile,
            tile,
            tile,
            pltpu.VMEM((96 * OWN, 3 * PMAX), jnp.bfloat16),
            pltpu.VMEM((24 * OWN, PMAX), f32),
            pltpu.VMEM((24 * OWN, PMAX), f32),
            pltpu.VMEM((OWN, 8, 128), f32),
            pltpu.VMEM((TABLE, 8, 128), f32),
            pltpu.VMEM((SENT * GROUPS, 8, 128), f32),
            pltpu.VMEM((OWN, 8, 128), f32),
            pltpu.VMEM((OWN, 8, 128), f32),
            pltpu.VMEM((3 * GROUPS, 8, 128), f32),
            pltpu.VMEM((3 * GROUPS, 8, 128), f32),
            pltpu.VMEM((TABLE, 8, 128), f32),
            pltpu.VMEM((OWN, 8, 128), f32),
            tile,
            tile,
            pltpu.SemaphoreType.DMA((2, 2, GROUPS)),
            pltpu.SemaphoreType.DMA((2, 2, GROUPS)),
            pltpu.SemaphoreType.DMA((12,)),
        ],
        compiler_params=pltpu.CompilerParams(
            collective_id=0, has_side_effects=True, vmem_limit_bytes=62 * 1024 * 1024
        ),
        name="snow_steps",
    )(
        neighbours,
        send_rows,
        counts,
        base_cell.reshape(planar),
        offset,
        velocity,
        affine,
        strain,
        plastic.reshape(planar),
        particle_mass.reshape(planar),
        jnp.asarray(consts),
        jnp.asarray(folds, dtype=jnp.bfloat16),
    )
    outs = pl.pallas_call(
        hand_over,
        out_shape=shapes,
        in_specs=[hbm] * 5,
        out_specs=[hbm] * 5,
        scratch_shapes=[pltpu.VMEM(x.shape, f32) for x in shapes] + [pltpu.SemaphoreType.DMA((2, 5))],
        compiler_params=pltpu.CompilerParams(vmem_limit_bytes=62 * 1024 * 1024),
        name="hand_over",
    )(*outs)
    return tuple(outs[:4]) + (outs[4].reshape(PARTICLES),)


def solution(mesh):
    length = mesh.shape["dom"]
    wide = P(None, "dom")
    flat = P("dom")
    return jax.shard_map(
        lambda *args: on_device(length, *args),
        mesh=mesh,
        in_specs=(flat, wide, wide, wide, wide, flat, flat, flat, P("dom", None), P("dom", None)),
        out_specs=(wide, wide, wide, wide, flat),
        check_vma=False,
    )
```
